256 devices in a mesh: ctx: 32 (over y, x, core), tp: 8 (over z).
Axes of the slice: x: 4, y: 4, z: 8, core: 2. Of those that a mesh axis runs over, the one named last changes fastest.
Arguments:
- query_rows: bfloat16 [1, 32, 512, 4096], P(None, 'ctx', None, 'tp'), may hold values from -200 to 200
- key_rows: bfloat16 [1, 32, 512, 1024], P(None, 'ctx', None, 'tp'), may hold values from -8 to 8
- value_rows: bfloat16 [1, 32, 512, 1024], P(None, 'ctx', None, 'tp'), may hold values from -12 to 12
- block_choice: int32 [1, 32, 512, 8, 3], P(None, 'ctx', None, 'tp'), may hold values from 0 to 31, as said below
- out_weight: bfloat16 [4096, 4096], P('tp'), may hold values from -0.1875 to 0.1875
- residual: bfloat16 [1, 32, 512, 4096], P(None, 'ctx', 'tp'), may hold values from -3 to 3
Outputs:
- mixed: bfloat16 [1, 32, 512, 4096], P(None, 'ctx', 'tp')
The draws below stay inside these ranges and needn't reach their ends.
Inputs may be any that keep to these rules, and one draw needn't show every extreme that they name: `block_choice`: entry 0 is the token's own block; block s lies on device s % 32. For one device and key head, its tokens form groups of 128 consecutive tokens that share entries 1 and 2. Each of these entries names an earlier block or repeats the token's own block (which then adds nothing). No other device is named by more than one group and entry of the same device and key head, so at most 128 tokens of one device and key head read blocks on any one other device, and exactly 128 do for some pair in every draw.
All inputs are finite; a program needn't handle non-finite values.
Results may differ from the reference program's by a relative error of at most 0.015.
Values may be sent and summed in bfloat16 or wider, within the bound.
A program may use at most 128 MiB of HBM per device.

```python
import math
import jax
import jax.numpy as jnp
from jax import lax

D = 4096
H = 32
KVH = 8
HD = 128
BLK = 512
TOP = 3
BPD = 1
SEQ = 16384
CAP = 128
N_CTX = 32
N_TP = 8


def choice_table(key):
    key = jax.random.fold_in(key, 11)
    device_ids = jnp.arange(N_CTX, dtype=jnp.int32)
    source = device_ids[:, None, None]
    other = device_ids[None, None, :]
    priority = jax.random.randint(jax.random.fold_in(key, 1), (N_CTX, KVH, N_CTX), 0, 4 * N_CTX)
    priority = jnp.where(other < source, priority, 8 * N_CTX + other)
    ordering = jnp.argsort(priority * N_CTX + other, axis=-1).astype(jnp.int32)
    group_scores = jax.random.randint(jax.random.fold_in(key, 2), (N_CTX, KVH, 4), 0, 64)
    group_rank = jnp.argsort(group_scores * 4 + jnp.arange(4, dtype=jnp.int32), axis=-1).astype(jnp.int32)
    rank = group_rank[:, :, :, None] + 4 * jnp.arange(2, dtype=jnp.int32)[None, None, None, :]
    picked = jnp.take_along_axis(ordering, jnp.minimum(rank, N_CTX - 1).reshape(N_CTX, KVH, 8), axis=2).reshape(N_CTX, KVH, 4, 2)
    active = rank < device_ids[:, None, None, None]
    own = jnp.broadcast_to(device_ids[:, None, None, None], (N_CTX, KVH, 4, 2))
    extra = jnp.where(active, picked, own)
    extra = jnp.repeat(jnp.transpose(extra, (0, 2, 1, 3)), CAP, axis=1)
    own_block = jnp.broadcast_to(device_ids[:, None, None, None], (N_CTX, BLK, KVH, 1))
    return jnp.concatenate([own_block, extra], axis=-1)[None].astype(jnp.int32)


def key_parts(key):
    key = jax.random.fold_in(key, 23)
    normal = jax.random.normal(jax.random.fold_in(key, 1), (BPD, N_CTX, BLK, KVH * HD), jnp.float32)
    return normal


def draw_block_choice(key, part):
    return choice_table(key)


def draw_key_rows(key, part):
    normal = key_parts(key)
    result = jnp.clip(1.2 * normal, -8.0, 8.0)
    return result.astype(jnp.bfloat16)


def draw_query_rows(key, part):
    key = jax.random.fold_in(key, 7)
    result = jnp.clip(1.2 * jax.random.normal(jax.random.fold_in(key, 1), (BPD, N_CTX, BLK, H * HD), jnp.float32), -8.0, 8.0)
    return result.astype(jnp.bfloat16)


def block_scale(own_key, dims, split, smallest, largest):
    level = 1.0
    for axis_at, blocks in split:
        steps = jax.random.uniform(jax.random.fold_in(jax.random.fold_in(own_key, 6), axis_at), (blocks,), jnp.float32, smallest / len(split), largest / len(split))
        level = level * jnp.repeat(jnp.exp(steps), dims[axis_at] // blocks).reshape((-1,) + (1,) * (len(dims) - 1 - axis_at))
    return level


def centred(stream_key, extent, scale, bound, shards=(), kind=jnp.bfloat16):
    factor_of = block_scale(stream_key, extent, shards, -0.22, 0.18) if shards else 1.0
    drawn = jax.random.normal(stream_key, extent, jnp.float32) * scale * factor_of
    return jnp.minimum(jnp.maximum(drawn, -bound), bound).astype(kind)


def setup_inputs(seed: int = 0) -> dict:
    keys = jax.random.split(jax.random.key(seed), 7)
    query_rows = draw_query_rows(jax.random.fold_in(keys[6], 71), 0)
    key_rows = draw_key_rows(jax.random.fold_in(keys[6], 71), 0)
    value_rows = centred(keys[2], (BPD, N_CTX, BLK, KVH * HD), 2.0, 12.0, ((1, 32), (3, 8)))
    block_choice = draw_block_choice(jax.random.fold_in(keys[6], 71), 0)
    out_weight = centred(keys[4], (H * HD, D), (H * HD // 4) ** -0.5, 0.1875, ((0, 8),))
    residual = centred(keys[5], (BPD, N_CTX, BLK, D), 0.5, 3.0, ((1, 32), (2, 8)))
    return {"query_rows": query_rows, "key_rows": key_rows, "value_rows": value_rows, "block_choice": block_choice, "out_weight": out_weight, "residual": residual}


def soft_pool(scores, allowed, values, pattern):
    masked = jnp.where(allowed, scores, -jnp.inf)
    peak = lax.optimization_barrier(jnp.max(masked, axis=-1, keepdims=True))
    weights = jnp.where(allowed, jnp.exp(masked - peak), 0.0)
    total = lax.optimization_barrier(jnp.sum(weights, axis=-1, keepdims=True))
    rounded = lax.optimization_barrier(weights.astype(jnp.bfloat16)).astype(jnp.float32)
    pooled = jnp.einsum(pattern, rounded, values.astype(jnp.float32)) / total
    return (pooled, (peak + jnp.log(total))[..., 0])

def reference(query_rows, key_rows, value_rows, block_choice, out_weight, residual):
    group_size = H // KVH
    nblocks = BPD * N_CTX
    scaling = 1.0 / math.sqrt(HD)
    queries = query_rows.reshape(nblocks, BLK, KVH, group_size, HD)
    keys_all = key_rows.reshape(nblocks, BLK, KVH, HD)
    values_all = value_rows.reshape(nblocks, BLK, KVH, HD)
    choices_all = block_choice.reshape(nblocks, BLK, KVH, TOP)
    positions = jnp.arange(BLK, dtype=jnp.int32)
    causal = (positions[:, None] >= positions[None, :])[:, None, None, :]

    def one_block(index):
        query_now = queries[index]
        own_scores = jnp.einsum('nkgd,mkd->nkgm', query_now.astype(jnp.float32), keys_all[index].astype(jnp.float32)) * scaling
        own_pooled, own_logsum = soft_pool(own_scores, causal, values_all[index], 'nkgm,mkd->nkgd')
        pooled_list = [own_pooled]
        logsum_list = [own_logsum]
        for entry in range(1, TOP):
            chosen = choices_all[index][:, :, entry].astype(jnp.int32)

            def one_head(head):
                picked = lax.dynamic_index_in_dim(chosen, head, 1, keepdims=False).astype(jnp.int32)
                keys_head = lax.dynamic_index_in_dim(keys_all, head, 2, keepdims=False)
                values_head = lax.dynamic_index_in_dim(values_all, head, 2, keepdims=False)
                far_keys = keys_head[picked].astype(jnp.float32)
                far_values = values_head[picked]
                query_head = lax.dynamic_index_in_dim(query_now, head, 1, keepdims=False).astype(jnp.float32)
                far_scores = jnp.einsum('ngd,nmd->ngm', query_head, far_keys) * scaling
                allowed = jnp.ones(far_scores.shape, dtype=bool)
                return soft_pool(far_scores, allowed, far_values, 'ngm,nmd->ngd')
            pooled, logsum = lax.map(one_head, jnp.arange(KVH, dtype=jnp.int32))
            pooled = jnp.moveaxis(pooled, 0, 1)
            logsum = jnp.moveaxis(logsum, 0, 1)
            usable = (chosen != index)[:, :, None]
            pooled_list.append(pooled)
            logsum_list.append(jnp.where(usable, logsum, -jnp.inf))
        stacked_logsum = jnp.stack(logsum_list, axis=0)
        stacked_pooled = jnp.stack(pooled_list, axis=0)
        top_logsum = lax.optimization_barrier(jnp.max(stacked_logsum, axis=0))
        scales = jnp.exp(stacked_logsum - top_logsum)
        merged = lax.optimization_barrier(jnp.sum(scales[..., None] * stacked_pooled, axis=0)) / lax.optimization_barrier(jnp.sum(scales, axis=0))[..., None]
        return merged.astype(jnp.bfloat16).reshape(BLK, H * HD)
    attention = lax.map(one_block, jnp.arange(nblocks, dtype=jnp.int32))
    flat = attention.reshape(SEQ, H * HD)
    width = H * HD // N_TP
    total = residual.reshape(SEQ, D).astype(jnp.float32)
    for shard in range(N_TP):
        part = jnp.dot(flat[:, shard * width:(shard + 1) * width], out_weight[shard * width:(shard + 1) * width], preferred_element_type=jnp.float32)
        total = total + lax.optimization_barrier(part.astype(jnp.bfloat16)).astype(jnp.float32)
    return total.astype(jnp.bfloat16).reshape(BPD, N_CTX, BLK, D)
```

```python
import functools
import math

import jax
import jax.numpy as jnp
from jax import lax
from jax.experimental import pallas as pl
from jax.experimental.pallas import tpu as pltpu
from jax.sharding import PartitionSpec as P

MESH = pl.DeviceIdType.MESH
HD = 128
HEADS = 4
BLK = 512
NX, NY, NZ = 4, 4, 8
WIDTH = 4096
HALF = 2048
QUART = 1024
CHUNKS = 8
NEG = -1e30
EXP2 = math.log2(math.e) / math.sqrt(HD)


def kernel(
    choice, q_ref, k_ref, v_ref, w_hbm, res_ref, out_ref,
    kv, w, own_acc, own_max, own_sum, att_send, att_in, part, rin0, rin, fin_send, fin_in,
    w_sem, y_send, y_recv, x_send, x_recv, a_send, a_recv, r_send, r_recv, f_send, f_recv,
):
    c = lax.axis_index("ctx")
    z = lax.axis_index("tp")
    core = lax.rem(c, 2)
    x = lax.rem(c // 2, NX)
    y = c // (2 * NX)

    def index(xx, yy, cc):
        return (yy * NX + xx) * 2 + cc

    x_next, x_prev = lax.rem(x + 1, NX), lax.rem(x + NX - 1, NX)
    x_far = lax.rem(x + 2, NX)
    right = (index(x_next, y, core), z)
    left = (index(x_prev, y, core), z)
    sibling = (index(x, y, 1 - core), z)
    up = (c, lax.rem(z + 1, NZ))
    down = (c, lax.rem(z + NZ - 1, NZ))

    def row(yy):
        return (index(x, yy, core), z)

    def remote(src, dst, s_sem, r_sem, device):
        return pltpu.make_async_remote_copy(
            src_ref=src, dst_ref=dst, send_sem=s_sem, recv_sem=r_sem, device_id=device, device_id_type=MESH
        )

    barrier = pltpu.get_barrier_semaphore()
    for device in (right, left, sibling, up, down):
        pl.semaphore_signal(barrier, inc=1, device_id=device, device_id_type=MESH)
    for step in range(1, NY):
        pl.semaphore_signal(barrier, inc=1, device_id=row(lax.rem(y + step, NY)), device_id_type=MESH)
    w_copy = pltpu.make_async_copy(w_hbm, w, w_sem)
    w_copy.start()
    kv[c, 0] = k_ref[...]
    kv[c, 1] = v_ref[...]
    pl.semaphore_wait(barrier, 8)

    def y_copy(step):
        target = lax.rem(y + step, NY)
        return remote(kv.at[c], kv.at[c], y_send.at[step - 1], y_recv.at[y], row(target))

    def y_arrival(layer):
        b = index(x, layer, core)
        return remote(kv.at[b], kv.at[b], y_send.at[0], y_recv.at[layer], row(lax.rem(y + 1, NY)))

    def blocks(j, cc):
        layer = y - j
        return [index(xx, layer, cc) for xx in (x, x_prev, x_next, x_far)]

    def x_copy(j, n, src, device):
        return remote(src, src, x_send.at[j, n], x_recv.at[j, n], device)

    def x_send_copy(j, n):
        mine, prev, nxt, far = blocks(j, core)
        src = [kv.at[mine], kv.at[mine], kv.at[mine], kv.at[prev, 0], kv.at[nxt, 1],
               kv.at[prev], kv.at[nxt], kv.at[far]][n]
        return x_copy(j, n, src, [right, left, sibling, right, left, sibling, sibling, sibling][n])

    def x_arrival(j, n):
        mine, prev, nxt, far = blocks(j, core)
        s_mine, s_prev, s_nxt, s_far = blocks(j, 1 - core)
        ref = [kv.at[prev], kv.at[nxt], kv.at[s_mine], kv.at[far, 0], kv.at[far, 1],
               kv.at[s_prev], kv.at[s_nxt], kv.at[s_far]][n]
        return x_copy(j, n, ref, sibling)

    def gather_0(j):
        @pl.when((j >= 0) & (j <= y))
        def _():
            @pl.when(j >= 1)
            def _():
                y_arrival(y - j).wait_recv()
            for n in (0, 1, 2):
                x_send_copy(j, n).start()

    def gather_1(j):
        @pl.when((j >= 0) & (j <= y))
        def _():
            x_arrival(j, 0).wait_recv()
            x_send_copy(j, 3).start()
            x_send_copy(j, 5).start()
            x_arrival(j, 1).wait_recv()
            x_send_copy(j, 4).start()
            x_send_copy(j, 6).start()

    def gather_2(j):
        @pl.when((j >= 0) & (j <= y))
        def _():
            x_arrival(j, 3).wait_recv()
            x_arrival(j, 4).wait_recv()
            x_send_copy(j, 7).start()

    def gather(n):
        gather_1(n - 1)
        gather_0(n)
        gather_2(n - 2)

    gather_0(jnp.int32(0))
    for step in range(1, NY):
        @pl.when(y + step < NY)
        def _():
            y_copy(step).start()

    def stacked(r, g):
        rows = []
        for h in range(HEADS):
            for u in (2 * g, 2 * g + 1):
                start = pl.multiple_of(64 * u + 16 * r, 16)
                rows.append(q_ref[pl.ds(start, 16), h * HD:(h + 1) * HD])
        return jnp.concatenate(rows, axis=0)

    def scores(qs, keys):
        return lax.dot_general(qs, keys, (((1,), (1,)), ((), ())), preferred_element_type=jnp.float32)

    def own_quarter(r, carry):
        for g in range(4):
            keys = 128 * (g + 1)
            s = scores(stacked(r, g), k_ref[0:keys, :])
            a = lax.broadcasted_iota(jnp.int32, (128, keys), 0)
            token = 128 * g + 64 * (lax.rem(a, 32) // 16) + 16 * r + lax.rem(a, 16)
            key = lax.broadcasted_iota(jnp.int32, (128, keys), 1)
            s = jnp.where(key <= token, s, NEG)
            m = jnp.max(s, axis=1, keepdims=True)
            p = jnp.exp2((s - m) * EXP2)
            n = r * 4 + g
            own_max[n] = m
            own_sum[n] = jnp.sum(p, axis=1, keepdims=True)
            own_acc[n] = jnp.dot(p.astype(jnp.bfloat16), v_ref[0:keys, :], preferred_element_type=jnp.float32)
        return carry

    lax.fori_loop(0, 4, own_quarter, 0)

    def a_copy(r):
        return remote(att_send.at[r], att_in.at[y], a_send.at[r], a_recv.at[y], row(r))

    def a_arrival(k):
        return remote(att_in.at[k], att_in.at[k], a_send.at[0], a_recv.at[k], row(lax.rem(y + 1, NY)))

    def far_attention():
        def wait_layer(j, carry):
            for n in (2, 5, 6, 7):
                x_arrival(j, n).wait_recv()
            return carry

        lax.fori_loop(0, y + 1, wait_layer, 0)

        def far_quarter(step, carry):
            r = lax.rem(y + 1 + step, NY)
            for g in range(4):
                qs = stacked(r, g)
                n = r * 4 + g
                s = []
                values = []
                for e in range(2):
                    b = choice[2 * g + e]
                    bias = jnp.where(b != c, 0.0, NEG).astype(jnp.float32)
                    s.append(scores(qs, kv[b, 0]) + bias)
                    values.append(kv[b, 1])
                m_own = own_max[n]
                m = jnp.maximum(
                    m_own, jnp.maximum(jnp.max(s[0], axis=1, keepdims=True), jnp.max(s[1], axis=1, keepdims=True))
                )
                scale = jnp.exp2((m_own - m) * EXP2)
                total = own_sum[n] * scale
                acc = own_acc[n] * scale
                for e in range(2):
                    p = jnp.exp2((s[e] - m) * EXP2)
                    total = total + jnp.sum(p, axis=1, keepdims=True)
                    acc = acc + jnp.dot(p.astype(jnp.bfloat16), values[e], preferred_element_type=jnp.float32)
                result = (acc / total).astype(jnp.bfloat16)
                for h in range(HEADS):
                    att_send[r, 32 * g:32 * g + 32, h * HD:(h + 1) * HD] = result[32 * h:32 * h + 32]

            @pl.when(r != y)
            def _():
                a_copy(r).start()

            @pl.when(r == y)
            def _():
                att_in[y] = att_send[r]
            return carry

        lax.fori_loop(0, NY, far_quarter, 0)

    def r_copy(n, way, stage, src, dst):
        return remote(src, dst, r_send.at[n, way, stage], r_recv.at[n, way, stage], up if way == 0 else down)

    def shard(step):
        return lax.rem(z + step, NZ)

    def stage_0(n):
        k, h = n // 2, lax.rem(n, 2)

        @pl.when((h == 0) & (k != y))
        def _():
            a_arrival(k).wait_recv()

        columns = pl.ds(pl.multiple_of(h * HALF, HALF), HALF)
        product = jnp.dot(att_in[k], w[:, columns], preferred_element_type=jnp.float32)
        part[n] = product.astype(jnp.bfloat16).reshape(NZ, 16, HALF)
        r_copy(n, 0, 0, part.at[n, shard(4), :, pl.ds(0, QUART)], rin0.at[n, 0]).start()
        r_copy(n, 1, 0, part.at[n, shard(4), :, pl.ds(QUART, QUART)], rin0.at[n, 1]).start()

    def stage_1(n):
        for way, step in ((0, 3), (1, 5)):
            d = shard(step)
            columns = pl.ds(way * QUART, QUART)
            r_copy(n, way, 0, rin0.at[n, way], rin0.at[n, way]).wait_recv()
            total = part[n, d, :, columns].astype(jnp.float32) + rin0[n, way].astype(jnp.float32)
            part[n, d, :, columns] = total.astype(jnp.bfloat16)
            r_copy(n, way, 1, part.at[n, d], rin.at[n, way, 0]).start()

    def stage_mid(n, stage):
        for way, step in ((0, 4 - stage), (1, 4 + stage)):
            d = shard(step)
            r_copy(n, way, stage - 1, rin.at[n, way, stage - 2], rin.at[n, way, stage - 2]).wait_recv()
            total = part[n, d].astype(jnp.float32) + rin[n, way, stage - 2].astype(jnp.float32)
            part[n, d] = total.astype(jnp.bfloat16)
            r_copy(n, way, stage, part.at[n, d], rin.at[n, way, stage - 1]).start()

    def f_copy(k, h):
        return remote(fin_send.at[k, h], fin_in.at[y, h], f_send.at[k, h], f_recv.at[y, h], row(k))

    def f_arrival(r, h):
        return remote(fin_in.at[r, h], fin_in.at[r, h], f_send.at[0, h], f_recv.at[r, h], row(lax.rem(y + 1, NY)))

    def stage_4(n):
        k, h = n // 2, lax.rem(n, 2)
        for way in range(2):
            r_copy(n, way, 3, rin.at[n, way, 2], rin.at[n, way, 2]).wait_recv()
        total = part[n, z].astype(jnp.float32) + rin[n, 0, 2].astype(jnp.float32) + rin[n, 1, 2].astype(jnp.float32)
        total = total.astype(jnp.bfloat16)

        @pl.when(k != y)
        def _():
            fin_send[k, h] = total
            f_copy(k, h).start()

        @pl.when(k == y)
        def _():
            fin_in[y, h] = total

    def tick(t):
        for stage, work in ((4, stage_4), (3, lambda n: stage_mid(n, 3)), (2, lambda n: stage_mid(n, 2)),
                            (1, stage_1), (0, stage_0)):
            n = t - stage

            @pl.when((n >= 0) & (n < CHUNKS))
            def _():
                work(n)

    gather(jnp.int32(1))
    w_copy.wait()

    def round_(step, carry):
        tick(step - 2)

        @pl.when(lax.rem(step, 2) == 0)
        def _():
            gather(step // 2 + 2)

            @pl.when(y == step // 2)
            def _():
                far_attention()
        return carry

    lax.fori_loop(0, CHUNKS + 4 + 2, round_, 0)

    for r in range(NY):
        for h in range(2):
            @pl.when(y != r)
            def _():
                f_arrival(r, h).wait_recv()
            rows, columns = pl.ds(16 * r, 16), pl.ds(h * HALF, HALF)
            total = res_ref[rows, columns].astype(jnp.float32) + fin_in[r, h].astype(jnp.float32)
            out_ref[rows, columns] = total.astype(jnp.bfloat16)

    for step in range(1, NY):
        @pl.when(y + step < NY)
        def _():
            y_copy(step).wait_send()

    def drain_layer(j, carry):
        for n in range(8):
            x_send_copy(j, n).wait_send()
        return carry

    lax.fori_loop(0, y + 1, drain_layer, 0)
    for r in range(NY):
        @pl.when(y != r)
        def _():
            a_copy(r).wait_send()
            for h in range(2):
                f_copy(r, h).wait_send()

    def drain_chunk(n, carry):
        for way in range(2):
            r_copy(n, way, 0, rin0.at[n, way], rin0.at[n, way]).wait_send()
            for stage in (1, 2, 3):
                r_copy(n, way, stage, rin.at[n, way, stage - 1], rin.at[n, way, stage - 1]).wait_send()
        return carry

    lax.fori_loop(0, CHUNKS, drain_chunk, 0)


def body(query_rows, key_rows, value_rows, block_choice, out_weight, residual):
    choice = block_choice[0, 0, ::BLK // 4, 0, 1:].reshape(8)
    q = query_rows.reshape(BLK, HEADS * HD)
    k = key_rows.reshape(BLK, HD)
    v = value_rows.reshape(BLK, HD)
    res = residual.reshape(BLK // NZ, WIDTH)
    vmem = pl.BlockSpec(memory_space=pltpu.VMEM)
    bf16, f32 = jnp.bfloat16, jnp.float32
    dma = pltpu.SemaphoreType.DMA
    out = pl.pallas_call(
        kernel,
        out_shape=jax.ShapeDtypeStruct((BLK // NZ, WIDTH), bf16),
        in_specs=[pl.BlockSpec(memory_space=pltpu.SMEM), vmem, vmem, vmem, pl.BlockSpec(memory_space=pl.ANY), vmem],
        out_specs=vmem,
        scratch_shapes=[
            pltpu.VMEM((2 * NX * NY, 2, BLK, HD), bf16),
            pltpu.VMEM((HEADS * HD, WIDTH), bf16),
            pltpu.VMEM((16, 128, HD), f32),
            pltpu.VMEM((16, 128, 1), f32),
            pltpu.VMEM((16, 128, 1), f32),
            pltpu.VMEM((NY, 128, HEADS * HD), bf16),
            pltpu.VMEM((NY, 128, HEADS * HD), bf16),
            pltpu.VMEM((CHUNKS, NZ, 16, HALF), bf16),
            pltpu.VMEM((CHUNKS, 2, 16, QUART), bf16),
            pltpu.VMEM((CHUNKS, 2, 3, 16, HALF), bf16),
            pltpu.VMEM((NY, 2, 16, HALF), bf16),
            pltpu.VMEM((NY, 2, 16, HALF), bf16),
            dma, dma((NY - 1,)), dma((NY,)), dma((NY, 8)), dma((NY, 8)), dma((NY,)), dma((NY,)),
            dma((CHUNKS, 2, 4)), dma((CHUNKS, 2, 4)), dma((NY, 2)), dma((NY, 2)),
        ],
        compiler_params=pltpu.CompilerParams(
            collective_id=1, has_side_effects=True, vmem_limit_bytes=48 * 1024 * 1024
        ),
        name="attention_mix",
    )(choice, q, k, v, out_weight, res)
    return out.reshape(1, 1, BLK // NZ, WIDTH)


def solution(mesh):
    placed = (
        P(None, "ctx", None, "tp"),
        P(None, "ctx", None, "tp"),
        P(None, "ctx", None, "tp"),
        P(None, "ctx", None, "tp", None),
        P("tp", None),
        P(None, "ctx", "tp", None),
    )
    return jax.shard_map(
        body, mesh=mesh, in_specs=placed, out_specs=P(None, "ctx", "tp", None), check_vma=False
    )
```

```python
import functools
import math

import jax
import jax.numpy as jnp
from jax import lax
from jax.experimental import pallas as pl
from jax.experimental.pallas import tpu as pltpu
from jax.sharding import PartitionSpec as P

MESH = pl.DeviceIdType.MESH
HD = 128
HEADS = 4
BLK = 512
NX, NY, NZ = 4, 4, 8
WIDTH = 4096
CHUNKS = 8
PER_ROW = CHUNKS // NY
HALF = WIDTH // PER_ROW
QUART = HALF // 2
SKEW = 1
NEG = -1e30
SHARE_AT = ((2, 1), (3, 2))
FAR_AT = (-1, -1, 2, 4)
EXP2 = math.log2(math.e) / math.sqrt(HD)


def kernel(
    choice_hbm, q_hbm, k_hbm, v_hbm, w_hbm, res_hbm, out_ref,
    choice, q_ref, res_ref, kv, w, own_acc, own_max, own_sum, att_send, att_in, part, rin0, rin, fin_send, fin_in,
    in_sem, y_send, y_recv, x_send, x_recv, a_send, a_recv, r_send, r_recv, f_send, f_recv,
):
    c = lax.axis_index("ctx")
    z = lax.axis_index("tp")
    core = lax.rem(c, 2)
    x = lax.rem(c // 2, NX)
    y = c // (2 * NX)

    def index(xx, yy, cc):
        return (yy * NX + xx) * 2 + cc

    x_next, x_prev = lax.rem(x + 1, NX), lax.rem(x + NX - 1, NX)
    x_far = lax.rem(x + 2, NX)
    right = (index(x_next, y, core), z)
    left = (index(x_prev, y, core), z)
    sibling = (index(x, y, 1 - core), z)
    up = (c, lax.rem(z + 1, NZ))
    down = (c, lax.rem(z + NZ - 1, NZ))

    def row(yy):
        return (index(x, yy, core), z)

    def remote(src, dst, s_sem, r_sem, device):
        return pltpu.make_async_remote_copy(
            src_ref=src, dst_ref=dst, send_sem=s_sem, recv_sem=r_sem, device_id=device, device_id_type=MESH
        )

    barrier = pltpu.get_barrier_semaphore()
    for device in (right, left, sibling, up, down):
        pl.semaphore_signal(barrier, inc=1, device_id=device, device_id_type=MESH)
    for step in range(1, NY):
        pl.semaphore_signal(barrier, inc=1, device_id=row(lax.rem(y + step, NY)), device_id_type=MESH)
    k_copy, v_copy, q_copy, w_copy, choice_copy, res_copy = [
        pltpu.make_async_copy(src, dst, in_sem.at[n])
        for n, (src, dst) in enumerate(
            [(k_hbm, kv.at[c, 0]), (v_hbm, kv.at[c, 1]), (q_hbm, q_ref), (w_hbm, w), (choice_hbm, choice),
             (res_hbm, res_ref)]
        )
    ]
    for copy in (k_copy, v_copy, q_copy, choice_copy):
        copy.start()
    pl.semaphore_wait(barrier, 8)

    def y_copy(far, n, layer, target):
        b = index(x_far if far else x, layer, core)
        return remote(kv.at[b], kv.at[b], y_send.at[far, n], y_recv.at[far, layer], row(target))

    def y_own(far, n):
        return y_copy(far, n, y, lax.rem(y + 1, NY) if n == 0 else NY - 1)

    def y_relay(far):
        return y_copy(far, 2, lax.rem(NY + 3 - y, NY), lax.rem(NY + 5 - y, NY))

    def y_wait(far, layer):
        y_copy(far, 0, layer, lax.rem(y + 1, NY)).wait_recv()

    def y_start(far):
        @pl.when(y < NY - 1)
        def _():
            y_own(far, 0).start()

        @pl.when(y == 0)
        def _():
            y_own(far, 1).start()

    def y_pass_on(far):
        @pl.when(y == 3)
        def _():
            y_wait(far, 0)

        @pl.when(y >= 2)
        def _():
            y_relay(far).start()

    def blocks(j, cc):
        layer = y - j
        return [index(xx, layer, cc) for xx in (x, x_prev, x_next, x_far)]

    def x_copy(j, n, src, device):
        return remote(src, src, x_send.at[j, n], x_recv.at[j, n], device)

    def x_send_copy(j, n):
        mine, prev, nxt, far = blocks(j, core)
        if n < 4 and j == 0:
            src, half = (k_hbm, 0) if n in (0, 3) else (v_hbm, 1)
            device = right if n in (0, 2) else left
            return remote(src, kv.at[mine, half], x_send.at[0, n], x_recv.at[0, n], device)
        src, device = [
            (kv.at[mine], right), (kv.at[mine], left), None, None,
            (kv.at[prev, 0], right), (kv.at[nxt, 1], left),
            (kv.at[mine], sibling), (kv.at[prev], sibling), (kv.at[nxt], sibling), (kv.at[far], sibling),
        ][n]
        return x_copy(j, n, src, device)

    def x_arrival(j, n):
        mine, prev, nxt, far = blocks(j, core)
        ref = [kv.at[prev, 0], kv.at[nxt, 1], kv.at[prev, 1], kv.at[nxt, 0], kv.at[far, 0], kv.at[far, 1]][n]
        return x_copy(j, n, ref, sibling)

    def x_block_arrival(j, n):
        _, prev, nxt, _ = blocks(j, core)
        return x_copy(j, n, kv.at[(prev, nxt)[n]], sibling)

    def sibling_arrival(j, n):
        return x_copy(j, 6 + n, kv.at[blocks(j, 1 - core)[n]], sibling)

    def gather_start(j):
        @pl.when(j <= y)
        def _():
            x_send_copy(j, 0).start()
            x_send_copy(j, 1).start()
            if j == 0:
                x_send_copy(j, 2).start()
                x_send_copy(j, 3).start()
                w_copy.start()
                res_copy.start()
                k_copy.wait()
                v_copy.wait()
            x_send_copy(j, 6).start()

    def gather_forward():
        x_arrival(0, 0).wait_recv()
        x_send_copy(0, 4).start()
        x_arrival(0, 1).wait_recv()
        x_send_copy(0, 5).start()

    def gather_share(j):
        @pl.when(j <= y)
        def _():
            if j == 0:
                x_arrival(j, 2).wait_recv()
            else:
                x_block_arrival(j, 0).wait_recv()
            x_send_copy(j, 7).start()
            if j == 0:
                x_arrival(j, 3).wait_recv()
            else:
                x_block_arrival(j, 1).wait_recv()
            x_send_copy(j, 8).start()
            if j == 0:
                x_arrival(j, 4).wait_recv()
                x_arrival(j, 5).wait_recv()
            elif j < 3:
                y_wait(1, y - j)
            x_send_copy(j, 9).start()

    gather_start(0)
    y_start(0)

    def stacked(quarters, g):
        rows = []
        for r in quarters:
            for h in range(HEADS):
                for u in (2 * g, 2 * g + 1):
                    start = pl.multiple_of(64 * u + 16 * r, 16)
                    rows.append(q_ref[pl.ds(start, 16), h * HD:(h + 1) * HD])
        return jnp.concatenate(rows, axis=0)

    def scores(qs, keys):
        return lax.dot_general(qs, keys, (((1,), (1,)), ((), ())), preferred_element_type=jnp.float32)

    def own_attention():
        a = lax.broadcasted_iota(jnp.int32, (4 * 128, 128), 0)
        token = 64 * (lax.rem(a, 32) // 16) + 16 * (a // 128) + lax.rem(a, 16)
        key = lax.broadcasted_iota(jnp.int32, (4 * 128, 128), 1)
        for g in range(4):
            qs = stacked(range(4), g)
            last, before = pl.ds(128 * g, 128), pl.ds(0, 128 * g)
            s = jnp.where(key <= token, scores(qs, kv[c, 0, last]), NEG)
            m = jnp.max(s, axis=1, keepdims=True)
            if g > 0:
                s_before = scores(qs, kv[c, 0, before])
                m = jnp.maximum(m, jnp.max(s_before, axis=1, keepdims=True))
            p = jnp.exp2((s - m) * EXP2)
            total = jnp.sum(p, axis=1, keepdims=True)
            acc = jnp.dot(p.astype(jnp.bfloat16), kv[c, 1, last], preferred_element_type=jnp.float32)
            if g > 0:
                p = jnp.exp2((s_before - m) * EXP2)
                total = total + jnp.sum(p, axis=1, keepdims=True)
                acc = acc + jnp.dot(p.astype(jnp.bfloat16), kv[c, 1, before], preferred_element_type=jnp.float32)
            own_max[g] = m
            own_sum[g] = total
            own_acc[g] = acc

    q_copy.wait()
    own_attention()

    def a_copy(r):
        return remote(att_send.at[r], att_in.at[y], a_send.at[r], a_recv.at[y], row(r))

    def a_arrival(k):
        return remote(att_in.at[k], att_in.at[k], a_send.at[0], a_recv.at[k], row(lax.rem(y + 1, NY)))

    def far_attention():
        def wait_layer(j, carry):
            for n in range(4):
                sibling_arrival(j, n).wait_recv()
            return carry

        lax.fori_loop(0, y + 1, wait_layer, 0)

        def far_pair(step, carry):
            pair = lax.rem(y // 2 + 1 + step, 2)
            quarters = [2 * pair, 2 * pair + 1]
            rows = pl.ds(pl.multiple_of(256 * pair, 256), 256)

            for g in range(4):
                qs = stacked(quarters, g)
                s, tops, biases, values = [], [], [], []
                for e in range(2):
                    b = choice[1 + e, 0, 128 * g]
                    bias = jnp.where(b != c, 0.0, NEG).astype(jnp.float32)
                    s.append(scores(qs, kv[b, 0]))
                    tops.append(jnp.max(s[e], axis=1, keepdims=True) + bias)
                    biases.append(bias)
                    values.append(kv[b, 1])
                m_own = own_max[g, rows]
                m = jnp.maximum(m_own, jnp.maximum(tops[0], tops[1]))
                scale = jnp.exp2((m_own - m) * EXP2)
                total = own_sum[g, rows] * scale
                acc = own_acc[g, rows] * scale
                for e in range(2):
                    p = jnp.exp2((s[e] - (m - biases[e])) * EXP2)
                    total = total + jnp.sum(p, axis=1, keepdims=True)
                    acc = acc + jnp.dot(p.astype(jnp.bfloat16), values[e], preferred_element_type=jnp.float32)
                result = (acc / total).astype(jnp.bfloat16)
                to = pl.ds(32 * g, 32)
                for n, r in enumerate(quarters):
                    for h in range(HEADS):
                        first = 128 * n + 32 * h
                        att_send[r, to, h * HD:(h + 1) * HD] = result[first:first + 32]
            for r in quarters:
                @pl.when(r != y)
                def _():
                    a_copy(r).start()

                @pl.when(r == y)
                def _():
                    att_in[y] = att_send[r]
            return carry

        lax.fori_loop(0, 2, far_pair, 0)

    def r_copy(n, way, stage, src, dst):
        return remote(src, dst, r_send.at[n, way, stage], r_recv.at[n, way, stage], up if way == 0 else down)

    def shard(step):
        return lax.rem(z + step, NZ)

    def stage_0(n):
        k, h = n // PER_ROW, lax.rem(n, PER_ROW)

        @pl.when((h == 0) & (k != y))
        def _():
            a_arrival(k).wait_recv()

        columns = pl.ds(pl.multiple_of(h * HALF, HALF), HALF)
        product = jnp.dot(att_in[k], w[:, columns], preferred_element_type=jnp.float32)
        part[n] = product.astype(jnp.bfloat16).reshape(NZ, 16, HALF)
        r_copy(n, 0, 0, part.at[n, shard(4), :, pl.ds(0, QUART)], rin0.at[n, 0]).start()
        r_copy(n, 1, 0, part.at[n, shard(4), :, pl.ds(QUART, QUART)], rin0.at[n, 1]).start()

    def stage_1(n):
        for way, step in ((0, 3), (1, 5)):
            d = shard(step)
            columns = pl.ds(way * QUART, QUART)
            r_copy(n, way, 0, rin0.at[n, way], rin0.at[n, way]).wait_recv()
            total = part[n, d, :, columns].astype(jnp.float32) + rin0[n, way].astype(jnp.float32)
            part[n, d, :, columns] = total.astype(jnp.bfloat16)
            r_copy(n, way, 1, part.at[n, d], rin.at[n, way, 0]).start()

    def stage_mid(n, stage):
        for way, step in ((0, 4 - stage), (1, 4 + stage)):
            d = shard(step)
            r_copy(n, way, stage - 1, rin.at[n, way, stage - 2], rin.at[n, way, stage - 2]).wait_recv()
            total = part[n, d].astype(jnp.float32) + rin[n, way, stage - 2].astype(jnp.float32)
            part[n, d] = total.astype(jnp.bfloat16)
            r_copy(n, way, stage, part.at[n, d], rin.at[n, way, stage - 1]).start()

    def f_copy(k, h):
        return remote(fin_send.at[k, h], fin_in.at[y, h], f_send.at[k, h], f_recv.at[y, h], row(k))

    def f_arrival(r, h):
        return remote(fin_in.at[r, h], fin_in.at[r, h], f_send.at[0, h], f_recv.at[r, h], row(lax.rem(y + 1, NY)))

    def stage_4(n):
        k, h = n // PER_ROW, lax.rem(n, PER_ROW)
        for way in range(2):
            r_copy(n, way, 3, rin.at[n, way, 2], rin.at[n, way, 2]).wait_recv()
        total = part[n, z].astype(jnp.float32) + rin[n, 0, 2].astype(jnp.float32) + rin[n, 1, 2].astype(jnp.float32)
        total = total.astype(jnp.bfloat16)

        @pl.when(k != y)
        def _():
            fin_send[k, h] = total
            f_copy(k, h).start()

        @pl.when(k == y)
        def _():
            fin_in[y, h] = total

    def tick(t):
        for stage, work in ((0, stage_0), (1, stage_1), (2, lambda n: stage_mid(n, 2)),
                            (3, lambda n: stage_mid(n, 3)), (4, stage_4)):
            n = t - SKEW * stage

            @pl.when((n >= 0) & (n < CHUNKS))
            def _():
                work(n)

    gather_forward()

    @pl.when(y >= 1)
    def _():
        y_wait(0, y - 1)
    y_pass_on(0)
    gather_start(1)
    w_copy.wait()
    choice_copy.wait()
    res_copy.wait()

    def round_(step, carry):
        t = step - 1
        tick(t)

        @pl.when(t == -1)
        def _():
            gather_share(0)
            y_start(1)

            @pl.when(y >= 2)
            def _():
                y_wait(0, y - 2)
            gather_start(2)
            gather_start(3)
            gather_share(1)
            y_pass_on(1)

        for j, at in SHARE_AT:
            @pl.when(t == at)
            def _():
                gather_share(j)

        far_at = sum(jnp.where(y == j, at, 0) for j, at in enumerate(FAR_AT))

        @pl.when(t == far_at)
        def _():
            far_attention()
        return carry

    lax.fori_loop(0, CHUNKS + 4 * SKEW + 1, round_, 0)

    for r in range(NY):
        for h in range(PER_ROW):
            @pl.when(y != r)
            def _():
                f_arrival(r, h).wait_recv()
            rows, columns = pl.ds(16 * r, 16), pl.ds(h * HALF, HALF)
            total = res_ref[rows, columns].astype(jnp.float32) + fin_in[r, h].astype(jnp.float32)
            out_ref[rows, columns] = total.astype(jnp.bfloat16)

    for far in range(2):
        @pl.when(y < NY - 1)
        def _():
            y_own(far, 0).wait_send()

        @pl.when(y == 0)
        def _():
            y_own(far, 1).wait_send()

        @pl.when(y >= 2)
        def _():
            y_relay(far).wait_send()
    for j in range(NY):
        @pl.when(j <= y)
        def _():
            for n in range(10) if j == 0 else (0, 1, 6, 7, 8, 9):
                x_send_copy(j, n).wait_send()
    for r in range(NY):
        @pl.when(y != r)
        def _():
            a_copy(r).wait_send()
            for h in range(PER_ROW):
                f_copy(r, h).wait_send()

    def drain_chunk(n, carry):
        for way in range(2):
            r_copy(n, way, 0, rin0.at[n, way], rin0.at[n, way]).wait_send()
            for stage in (1, 2, 3):
                r_copy(n, way, stage, rin.at[n, way, stage - 1], rin.at[n, way, stage - 1]).wait_send()
        return carry

    lax.fori_loop(0, CHUNKS, drain_chunk, 0)


def body(query_rows, key_rows, value_rows, block_choice, out_weight, residual):
    choice = jnp.transpose(block_choice, (0, 1, 4, 3, 2)).reshape(3, 1, BLK)
    q = query_rows.reshape(BLK, HEADS * HD)
    k = key_rows.reshape(BLK, HD)
    v = value_rows.reshape(BLK, HD)
    res = residual.reshape(BLK // NZ, WIDTH)
    vmem, hbm = pl.BlockSpec(memory_space=pltpu.VMEM), pl.BlockSpec(memory_space=pl.ANY)
    bf16, f32 = jnp.bfloat16, jnp.float32
    dma = pltpu.SemaphoreType.DMA
    out = pl.pallas_call(
        kernel,
        out_shape=jax.ShapeDtypeStruct((BLK // NZ, WIDTH), bf16),
        in_specs=[hbm] * 6,
        out_specs=vmem,
        scratch_shapes=[
            pltpu.SMEM((3, 1, BLK), jnp.int32),
            pltpu.VMEM((BLK, HEADS * HD), bf16),
            pltpu.VMEM((BLK // NZ, WIDTH), bf16),
            pltpu.VMEM((2 * NX * NY, 2, BLK, HD), bf16),
            pltpu.VMEM((HEADS * HD, WIDTH), bf16),
            pltpu.VMEM((4, BLK, HD), f32),
            pltpu.VMEM((4, BLK, 1), f32),
            pltpu.VMEM((4, BLK, 1), f32),
            pltpu.VMEM((NY, 128, HEADS * HD), bf16),
            pltpu.VMEM((NY, 128, HEADS * HD), bf16),
            pltpu.VMEM((CHUNKS, NZ, 16, HALF), bf16),
            pltpu.VMEM((CHUNKS, 2, 16, QUART), bf16),
            pltpu.VMEM((CHUNKS, 2, 3, 16, HALF), bf16),
            pltpu.VMEM((NY, PER_ROW, 16, HALF), bf16),
            pltpu.VMEM((NY, PER_ROW, 16, HALF), bf16),
            dma((6,)), dma((2, 3)), dma((2, NY)), dma((NY, 10)), dma((NY, 10)), dma((NY,)), dma((NY,)),
            dma((CHUNKS, 2, 4)), dma((CHUNKS, 2, 4)), dma((NY, PER_ROW)), dma((NY, PER_ROW)),
        ],
        compiler_params=pltpu.CompilerParams(
            collective_id=1, has_side_effects=True, vmem_limit_bytes=62 * 1024 * 1024
        ),
        name="attention_mix",
    )(choice, q, k, v, out_weight, res)
    return out.reshape(1, 1, BLK // NZ, WIDTH)


def solution(mesh):
    placed = (
        P(None, "ctx", None, "tp"),
        P(None, "ctx", None, "tp"),
        P(None, "ctx", None, "tp"),
        P(None, "ctx", None, "tp", None),
        P("tp", None),
        P(None, "ctx", "tp", None),
    )
    return jax.shard_map(
        body, mesh=mesh, in_specs=placed, out_specs=P(None, "ctx", "tp", None), check_vma=False
    )
```

```python
import functools
import math

import jax
import jax.numpy as jnp
from jax import lax
from jax.experimental import pallas as pl
from jax.experimental.pallas import tpu as pltpu
from jax.sharding import PartitionSpec as P

MESH = pl.DeviceIdType.MESH
HD = 128
HEADS = 4
BLK = 512
NX, NY, NZ = 4, 4, 8
WIDTH = 4096
CHUNKS = 8
PER_ROW = CHUNKS // NY
HALF = WIDTH // PER_ROW
QUART = HALF // 2
SKEW = 1
NEG = -1e30
SHARE_AT = ((2, 1), (3, 2))
FAR_AT = (-1, -1, 2, 4)
EXP2 = math.log2(math.e) / math.sqrt(HD)


def kernel(
    choice_hbm, q_hbm, k_hbm, v_hbm, w_hbm, res_hbm, out_ref,
    choice, q_ref, v_ref, res_ref, kv, w, own_acc, own_max, own_sum, att_send, att_in, part, rin0, rin, fin_send, fin_in,
    in_sem, y_send, y_recv, x_send, x_recv, a_send, a_recv, r_send, r_recv, f_send, f_recv,
):
    c = lax.axis_index("ctx")
    z = lax.axis_index("tp")
    core = lax.rem(c, 2)
    x = lax.rem(c // 2, NX)
    y = c // (2 * NX)

    def index(xx, yy, cc):
        return (yy * NX + xx) * 2 + cc

    x_next, x_prev = lax.rem(x + 1, NX), lax.rem(x + NX - 1, NX)
    x_far = lax.rem(x + 2, NX)
    right = (index(x_next, y, core), z)
    left = (index(x_prev, y, core), z)
    sibling = (index(x, y, 1 - core), z)
    up = (c, lax.rem(z + 1, NZ))
    down = (c, lax.rem(z + NZ - 1, NZ))

    def row(yy):
        return (index(x, yy, core), z)

    def remote(src, dst, s_sem, r_sem, device):
        return pltpu.make_async_remote_copy(
            src_ref=src, dst_ref=dst, send_sem=s_sem, recv_sem=r_sem, device_id=device, device_id_type=MESH
        )

    barrier = pltpu.get_barrier_semaphore()
    for device in (right, left, sibling, up, down):
        pl.semaphore_signal(barrier, inc=1, device_id=device, device_id_type=MESH)
    for step in range(1, NY):
        pl.semaphore_signal(barrier, inc=1, device_id=row(lax.rem(y + step, NY)), device_id_type=MESH)
    k_copy, v_copy, q_copy, w_copy, choice_copy, res_copy = [
        pltpu.make_async_copy(src, dst, in_sem.at[n])
        for n, (src, dst) in enumerate(
            [(k_hbm, kv.at[c, 0]), (v_hbm, v_ref), (q_hbm, q_ref), (w_hbm, w), (choice_hbm, choice),
             (res_hbm, res_ref)]
        )
    ]
    for copy in (k_copy, v_copy, q_copy, choice_copy):
        copy.start()
    pl.semaphore_wait(barrier, 8)

    def y_copy(far, n, layer, target):
        b = index(x_far if far else x, layer, core)
        return remote(kv.at[b], kv.at[b], y_send.at[far, n], y_recv.at[far, layer], row(target))

    def y_own(far, n):
        return y_copy(far, n, y, lax.rem(y + 1, NY) if n == 0 else NY - 1)

    def y_relay(far):
        return y_copy(far, 2, lax.rem(NY + 3 - y, NY), lax.rem(NY + 5 - y, NY))

    def y_wait(far, layer):
        y_copy(far, 0, layer, lax.rem(y + 1, NY)).wait_recv()

    def y_start(far):
        @pl.when(y < NY - 1)
        def _():
            y_own(far, 0).start()

        @pl.when(y == 0)
        def _():
            y_own(far, 1).start()

    def y_pass_on(far):
        @pl.when(y == 3)
        def _():
            y_wait(far, 0)

        @pl.when(y >= 2)
        def _():
            y_relay(far).start()

    def blocks(j, cc):
        layer = y - j
        return [index(xx, layer, cc) for xx in (x, x_prev, x_next, x_far)]

    def x_copy(j, n, src, device):
        return remote(src, src, x_send.at[j, n], x_recv.at[j, n], device)

    def x_send_copy(j, n):
        mine, prev, nxt, far = blocks(j, core)
        if n < 4 and j == 0:
            src, half = (k_hbm, 0) if n in (0, 3) else (kv.at[mine, 1], 1)
            device = right if n in (0, 2) else left
            return remote(src, kv.at[mine, half], x_send.at[0, n], x_recv.at[0, n], device)
        src, device = [
            (kv.at[mine], right), (kv.at[mine], left), None, None,
            (kv.at[prev, 0], right), (kv.at[nxt, 1], left),
            (kv.at[mine], sibling), (kv.at[prev], sibling), (kv.at[nxt], sibling), (kv.at[far], sibling),
        ][n]
        return x_copy(j, n, src, device)

    def x_arrival(j, n):
        mine, prev, nxt, far = blocks(j, core)
        ref = [kv.at[prev, 0], kv.at[nxt, 1], kv.at[prev, 1], kv.at[nxt, 0], kv.at[far, 0], kv.at[far, 1]][n]
        return x_copy(j, n, ref, sibling)

    def x_block_arrival(j, n):
        _, prev, nxt, _ = blocks(j, core)
        return x_copy(j, n, kv.at[(prev, nxt)[n]], sibling)

    def sibling_arrival(j, n):
        return x_copy(j, 6 + n, kv.at[blocks(j, 1 - core)[n]], sibling)

    def gather_start(j):
        @pl.when(j <= y)
        def _():
            x_send_copy(j, 0).start()
            if j == 0:
                x_send_copy(j, 3).start()
                v_copy.wait()
                for n in range(4):
                    part_rows = pl.ds(HD * n, HD)
                    kv[c, 1, part_rows] = v_ref[part_rows, :].T
            x_send_copy(j, 1).start()
            if j == 0:
                x_send_copy(j, 2).start()
                k_copy.wait()
                w_copy.start()
                res_copy.start()
            x_send_copy(j, 6).start()

    def gather_forward():
        x_arrival(0, 0).wait_recv()
        x_send_copy(0, 4).start()
        x_arrival(0, 1).wait_recv()
        x_send_copy(0, 5).start()

    def gather_share(j):
        @pl.when(j <= y)
        def _():
            if j == 0:
                x_arrival(j, 2).wait_recv()
            else:
                x_block_arrival(j, 0).wait_recv()
            x_send_copy(j, 7).start()
            if j == 0:
                x_arrival(j, 3).wait_recv()
            else:
                x_block_arrival(j, 1).wait_recv()
            x_send_copy(j, 8).start()
            if j == 0:
                x_arrival(j, 4).wait_recv()
                x_arrival(j, 5).wait_recv()
            elif j < 3:
                y_wait(1, y - j)
            x_send_copy(j, 9).start()

    gather_start(0)
    y_start(0)

    def stacked(quarters, g):
        rows = []
        for r in quarters:
            for h in range(HEADS):
                for u in (2 * g, 2 * g + 1):
                    start = pl.multiple_of(64 * u + 16 * r, 16)
                    rows.append(q_ref[pl.ds(start, 16), h * HD:(h + 1) * HD])
        return jnp.concatenate(rows, axis=0)

    def scores(qs, keys):
        return lax.dot_general(qs, keys, (((1,), (1,)), ((), ())), preferred_element_type=jnp.float32)

    def values(b, first, last):
        return jnp.concatenate([kv[b, 1, HD * n:HD * (n + 1)] for n in range(first, last)], axis=1)

    def own_attention():
        a = lax.broadcasted_iota(jnp.int32, (128, BLK), 1)
        token = 64 * (lax.rem(a, 32) // 16) + 16 * (a // 128) + lax.rem(a, 16)
        key = lax.broadcasted_iota(jnp.int32, (128, BLK), 0)
        for g in range(4):
            qs = stacked(range(4), g)
            last, before = pl.ds(128 * g, 128), pl.ds(0, 128 * g)
            s = jnp.where(key <= token, scores(kv[c, 0, last], qs), NEG)
            m = jnp.max(s, axis=0, keepdims=True)
            if g > 0:
                s_before = scores(kv[c, 0, before], qs)
                m = jnp.maximum(m, jnp.max(s_before, axis=0, keepdims=True))
            p = jnp.exp2((s - m) * EXP2)
            total = jnp.sum(p, axis=0, keepdims=True)
            acc = jnp.dot(values(c, g, g + 1), p.astype(jnp.bfloat16), preferred_element_type=jnp.float32)
            if g > 0:
                p = jnp.exp2((s_before - m) * EXP2)
                total = total + jnp.sum(p, axis=0, keepdims=True)
                acc = acc + jnp.dot(values(c, 0, g), p.astype(jnp.bfloat16), preferred_element_type=jnp.float32)
            own_max[g] = m
            own_sum[g] = total
            own_acc[g] = acc

    q_copy.wait()
    own_attention()

    def a_copy(r):
        return remote(att_send.at[r], att_in.at[y], a_send.at[r], a_recv.at[y], row(r))

    def a_arrival(k):
        return remote(att_in.at[k], att_in.at[k], a_send.at[0], a_recv.at[k], row(lax.rem(y + 1, NY)))

    def far_attention():
        def wait_layer(j, carry):
            for n in range(4):
                sibling_arrival(j, n).wait_recv()
            return carry

        lax.fori_loop(0, y + 1, wait_layer, 0)

        def far_pair(step, carry):
            pair = lax.rem(y // 2 + 1 + step, 2)
            quarters = [2 * pair, 2 * pair + 1]
            rows = pl.ds(pl.multiple_of(256 * pair, 256), 256)

            def group_scores(g):
                qs = stacked(quarters, g)
                return [scores(kv[choice[1 + e, 0, 128 * g], 0], qs) for e in range(2)]

            later = group_scores(0)
            for g in range(4):
                s = later
                if g < 3:
                    later = group_scores(g + 1)
                chosen = [choice[1 + e, 0, 128 * g] for e in range(2)]
                bias = [jnp.where(b != c, 0.0, NEG).astype(jnp.float32) for b in chosen]
                m_own = own_max[g, :, rows]
                m = m_own
                for e in range(2):
                    m = jnp.maximum(m, jnp.max(s[e], axis=0, keepdims=True) + bias[e])
                scale = jnp.exp2((m_own - m) * EXP2)
                total = own_sum[g, :, rows] * scale
                acc = own_acc[g, :, rows] * scale
                for e in range(2):
                    p = jnp.exp2((s[e] - (m - bias[e])) * EXP2)
                    total = total + jnp.sum(p, axis=0, keepdims=True)
                    acc = acc + jnp.dot(
                        values(chosen[e], 0, 4), p.astype(jnp.bfloat16), preferred_element_type=jnp.float32
                    )
                result = (acc * (1.0 / total)).T.astype(jnp.bfloat16)
                to = pl.ds(32 * g, 32)
                for n, r in enumerate(quarters):
                    for h in range(HEADS):
                        first = 128 * n + 32 * h
                        att_send[r, to, h * HD:(h + 1) * HD] = result[first:first + 32]
            for r in quarters:
                @pl.when(r != y)
                def _():
                    a_copy(r).start()

                @pl.when(r == y)
                def _():
                    att_in[y] = att_send[r]
            return carry

        lax.fori_loop(0, 2, far_pair, 0)

    def r_copy(n, way, stage, src, dst):
        return remote(src, dst, r_send.at[n, way, stage], r_recv.at[n, way, stage], up if way == 0 else down)

    def shard(step):
        return lax.rem(z + step, NZ)

    def stage_0(n):
        k, h = n // PER_ROW, lax.rem(n, PER_ROW)

        @pl.when((h == 0) & (k != y))
        def _():
            a_arrival(k).wait_recv()

        columns = pl.ds(pl.multiple_of(h * HALF, HALF), HALF)
        product = jnp.dot(att_in[k], w[:, columns], preferred_element_type=jnp.float32)
        part[n] = product.astype(jnp.bfloat16).reshape(NZ, 16, HALF)
        r_copy(n, 0, 0, part.at[n, shard(4), :, pl.ds(0, QUART)], rin0.at[n, 0]).start()
        r_copy(n, 1, 0, part.at[n, shard(4), :, pl.ds(QUART, QUART)], rin0.at[n, 1]).start()

    def stage_1(n):
        for way, step in ((0, 3), (1, 5)):
            d = shard(step)
            columns = pl.ds(way * QUART, QUART)
            r_copy(n, way, 0, rin0.at[n, way], rin0.at[n, way]).wait_recv()
            total = part[n, d, :, columns].astype(jnp.float32) + rin0[n, way].astype(jnp.float32)
            part[n, d, :, columns] = total.astype(jnp.bfloat16)
            r_copy(n, way, 1, part.at[n, d], rin.at[n, way, 0]).start()

    def stage_mid(n, stage):
        for way, step in ((0, 4 - stage), (1, 4 + stage)):
            d = shard(step)
            r_copy(n, way, stage - 1, rin.at[n, way, stage - 2], rin.at[n, way, stage - 2]).wait_recv()
            total = part[n, d].astype(jnp.float32) + rin[n, way, stage - 2].astype(jnp.float32)
            part[n, d] = total.astype(jnp.bfloat16)
            r_copy(n, way, stage, part.at[n, d], rin.at[n, way, stage - 1]).start()

    def f_copy(k, h):
        return remote(fin_send.at[k, h], fin_in.at[y, h], f_send.at[k, h], f_recv.at[y, h], row(k))

    def f_arrival(r, h):
        return remote(fin_in.at[r, h], fin_in.at[r, h], f_send.at[0, h], f_recv.at[r, h], row(lax.rem(y + 1, NY)))

    def stage_4(n):
        k, h = n // PER_ROW, lax.rem(n, PER_ROW)
        for way in range(2):
            r_copy(n, way, 3, rin.at[n, way, 2], rin.at[n, way, 2]).wait_recv()
        total = part[n, z].astype(jnp.float32) + rin[n, 0, 2].astype(jnp.float32) + rin[n, 1, 2].astype(jnp.float32)
        total = total.astype(jnp.bfloat16)

        @pl.when(k != y)
        def _():
            fin_send[k, h] = total
            f_copy(k, h).start()

        @pl.when(k == y)
        def _():
            fin_in[y, h] = total

    def tick(t):
        for stage, work in ((0, stage_0), (1, stage_1), (2, lambda n: stage_mid(n, 2)),
                            (3, lambda n: stage_mid(n, 3)), (4, stage_4)):
            n = t - SKEW * stage

            @pl.when((n >= 0) & (n < CHUNKS))
            def _():
                work(n)

    gather_forward()

    @pl.when(y >= 1)
    def _():
        y_wait(0, y - 1)
    y_pass_on(0)
    gather_start(1)
    w_copy.wait()
    choice_copy.wait()
    res_copy.wait()

    def round_(step, carry):
        t = step - 1
        tick(t)

        @pl.when(t == -1)
        def _():
            gather_share(0)
            y_start(1)

            @pl.when(y >= 2)
            def _():
                y_wait(0, y - 2)
            gather_start(2)
            gather_start(3)
            gather_share(1)
            y_pass_on(1)

        for j, at in SHARE_AT:
            @pl.when(t == at)
            def _():
                gather_share(j)

        far_at = sum(jnp.where(y == j, at, 0) for j, at in enumerate(FAR_AT))

        @pl.when(t == far_at)
        def _():
            far_attention()
        return carry

    lax.fori_loop(0, CHUNKS + 4 * SKEW + 1, round_, 0)

    for r in range(NY):
        for h in range(PER_ROW):
            @pl.when(y != r)
            def _():
                f_arrival(r, h).wait_recv()
            rows, columns = pl.ds(16 * r, 16), pl.ds(h * HALF, HALF)
            total = res_ref[rows, columns].astype(jnp.float32) + fin_in[r, h].astype(jnp.float32)
            out_ref[rows, columns] = total.astype(jnp.bfloat16)

    for far in range(2):
        @pl.when(y < NY - 1)
        def _():
            y_own(far, 0).wait_send()

        @pl.when(y == 0)
        def _():
            y_own(far, 1).wait_send()

        @pl.when(y >= 2)
        def _():
            y_relay(far).wait_send()
    for j in range(NY):
        @pl.when(j <= y)
        def _():
            for n in range(10) if j == 0 else (0, 1, 6, 7, 8, 9):
                x_send_copy(j, n).wait_send()
    for r in range(NY):
        @pl.when(y != r)
        def _():
            a_copy(r).wait_send()
            for h in range(PER_ROW):
                f_copy(r, h).wait_send()

    def drain_chunk(n, carry):
        for way in range(2):
            r_copy(n, way, 0, rin0.at[n, way], rin0.at[n, way]).wait_send()
            for stage in (1, 2, 3):
                r_copy(n, way, stage, rin.at[n, way, stage - 1], rin.at[n, way, stage - 1]).wait_send()
        return carry

    lax.fori_loop(0, CHUNKS, drain_chunk, 0)


def body(query_rows, key_rows, value_rows, block_choice, out_weight, residual):
    choice = jnp.transpose(block_choice, (0, 1, 4, 3, 2)).reshape(3, 1, BLK)
    q = query_rows.reshape(BLK, HEADS * HD)
    k = key_rows.reshape(BLK, HD)
    v = value_rows.reshape(BLK, HD)
    res = residual.reshape(BLK // NZ, WIDTH)
    vmem, hbm = pl.BlockSpec(memory_space=pltpu.VMEM), pl.BlockSpec(memory_space=pl.ANY)
    bf16, f32 = jnp.bfloat16, jnp.float32
    dma = pltpu.SemaphoreType.DMA
    out = pl.pallas_call(
        kernel,
        out_shape=jax.ShapeDtypeStruct((BLK // NZ, WIDTH), bf16),
        in_specs=[hbm] * 6,
        out_specs=vmem,
        scratch_shapes=[
            pltpu.SMEM((3, 1, BLK), jnp.int32),
            pltpu.VMEM((BLK, HEADS * HD), bf16),
            pltpu.VMEM((BLK, HD), bf16),
            pltpu.VMEM((BLK // NZ, WIDTH), bf16),
            pltpu.VMEM((2 * NX * NY, 2, BLK, HD), bf16),
            pltpu.VMEM((HEADS * HD, WIDTH), bf16),
            pltpu.VMEM((4, HD, BLK), f32),
            pltpu.VMEM((4, 1, BLK), f32),
            pltpu.VMEM((4, 1, BLK), f32),
            pltpu.VMEM((NY, 128, HEADS * HD), bf16),
            pltpu.VMEM((NY, 128, HEADS * HD), bf16),
            pltpu.VMEM((CHUNKS, NZ, 16, HALF), bf16),
            pltpu.VMEM((CHUNKS, 2, 16, QUART), bf16),
            pltpu.VMEM((CHUNKS, 2, 3, 16, HALF), bf16),
            pltpu.VMEM((NY, PER_ROW, 16, HALF), bf16),
            pltpu.VMEM((NY, PER_ROW, 16, HALF), bf16),
            dma((6,)), dma((2, 3)), dma((2, NY)), dma((NY, 10)), dma((NY, 10)), dma((NY,)), dma((NY,)),
            dma((CHUNKS, 2, 4)), dma((CHUNKS, 2, 4)), dma((NY, PER_ROW)), dma((NY, PER_ROW)),
        ],
        compiler_params=pltpu.CompilerParams(
            collective_id=1, has_side_effects=True, vmem_limit_bytes=62 * 1024 * 1024
        ),
        name="attention_mix",
    )(choice, q, k, v, out_weight, res)
    return out.reshape(1, 1, BLK // NZ, WIDTH)


def solution(mesh):
    placed = (
        P(None, "ctx", None, "tp"),
        P(None, "ctx", None, "tp"),
        P(None, "ctx", None, "tp"),
        P(None, "ctx", None, "tp", None),
        P("tp", None),
        P(None, "ctx", "tp", None),
    )
    return jax.shard_map(
        body, mesh=mesh, in_specs=placed, out_specs=P(None, "ctx", "tp", None), check_vma=False
    )
```

```python
import functools
import math

import jax
import jax.numpy as jnp
from jax import lax
from jax.experimental import pallas as pl
from jax.experimental.pallas import tpu as pltpu
from jax.sharding import PartitionSpec as P

MESH = pl.DeviceIdType.MESH
HD = 128
HEADS = 4
BLK = 512
NX, NY, NZ = 4, 4, 8
WIDTH = 4096
CHUNKS = 8
PER_ROW = CHUNKS // NY
HALF = WIDTH // PER_ROW
QUART = HALF // 2
SKEW = 1
NEG = -1e30
SHARE_AT = ((2, 1), (3, 2))
FAR_AT = (-1, -1, 2, 4)
EXP2 = math.log2(math.e) / math.sqrt(HD)


def kernel(
    choice_hbm, q_hbm, k_hbm, v_hbm, w_hbm, res_hbm, out_ref,
    choice, q_ref, v_ref, res_ref, kv, w, own_acc, own_max, own_sum, att_send, att_in, part, rin0, rin, fin_send, fin_in,
    in_sem, y_send, y_recv, x_send, x_recv, a_send, a_recv, r_send, r_recv, f_send, f_recv,
):
    c = lax.axis_index("ctx")
    z = lax.axis_index("tp")
    core = lax.rem(c, 2)
    x = lax.rem(c // 2, NX)
    y = c // (2 * NX)

    def index(xx, yy, cc):
        return (yy * NX + xx) * 2 + cc

    x_next, x_prev = lax.rem(x + 1, NX), lax.rem(x + NX - 1, NX)
    x_far = lax.rem(x + 2, NX)
    right = (index(x_next, y, core), z)
    left = (index(x_prev, y, core), z)
    sibling = (index(x, y, 1 - core), z)
    up = (c, lax.rem(z + 1, NZ))
    down = (c, lax.rem(z + NZ - 1, NZ))

    def row(yy):
        return (index(x, yy, core), z)

    def remote(src, dst, s_sem, r_sem, device):
        return pltpu.make_async_remote_copy(
            src_ref=src, dst_ref=dst, send_sem=s_sem, recv_sem=r_sem, device_id=device, device_id_type=MESH
        )

    barrier = pltpu.get_barrier_semaphore()
    for device in (right, left, sibling, up, down):
        pl.semaphore_signal(barrier, inc=1, device_id=device, device_id_type=MESH)
    for step in range(1, NY):
        pl.semaphore_signal(barrier, inc=1, device_id=row(lax.rem(y + step, NY)), device_id_type=MESH)
    k_copy, v_copy, q_copy, w_copy, choice_copy, res_copy = [
        pltpu.make_async_copy(src, dst, in_sem.at[n])
        for n, (src, dst) in enumerate(
            [(k_hbm, kv.at[c, 0]), (v_hbm, v_ref), (q_hbm, q_ref), (w_hbm, w), (choice_hbm, choice),
             (res_hbm, res_ref)]
        )
    ]
    for copy in (k_copy, v_copy, q_copy, choice_copy):
        copy.start()
    pl.semaphore_wait(barrier, 8)

    def y_copy(far, n, layer, target):
        b = index(x_far if far else x, layer, core)
        return remote(kv.at[b], kv.at[b], y_send.at[far, n], y_recv.at[far, layer], row(target))

    def y_own(far, n):
        return y_copy(far, n, y, lax.rem(y + 1, NY) if n == 0 else NY - 1)

    def y_relay(far):
        return y_copy(far, 2, lax.rem(NY + 3 - y, NY), lax.rem(NY + 5 - y, NY))

    def y_wait(far, layer):
        y_copy(far, 0, layer, lax.rem(y + 1, NY)).wait_recv()

    def y_start(far):
        @pl.when(y < NY - 1)
        def _():
            y_own(far, 0).start()

        @pl.when(y == 0)
        def _():
            y_own(far, 1).start()

    def y_pass_on(far):
        @pl.when(y == 3)
        def _():
            y_wait(far, 0)

        @pl.when(y >= 2)
        def _():
            y_relay(far).start()

    def blocks(j, cc):
        layer = y - j
        return [index(xx, layer, cc) for xx in (x, x_prev, x_next, x_far)]

    def x_copy(j, n, src, device):
        return remote(src, src, x_send.at[j, n], x_recv.at[j, n], device)

    def x_send_copy(j, n):
        mine, prev, nxt, far = blocks(j, core)
        if n < 4 and j == 0:
            src, half = (k_hbm, 0) if n in (0, 3) else (kv.at[mine, 1], 1)
            device = right if n in (0, 2) else left
            return remote(src, kv.at[mine, half], x_send.at[0, n], x_recv.at[0, n], device)
        src, device = [
            (kv.at[mine], right), (kv.at[mine], left), None, None,
            (kv.at[prev, 0], right), (kv.at[nxt, 1], left),
            (kv.at[mine], sibling), (kv.at[prev], sibling), (kv.at[nxt], sibling), (kv.at[far], sibling),
        ][n]
        return x_copy(j, n, src, device)

    def x_arrival(j, n):
        mine, prev, nxt, far = blocks(j, core)
        ref = [kv.at[prev, 0], kv.at[nxt, 1], kv.at[prev, 1], kv.at[nxt, 0], kv.at[far, 0], kv.at[far, 1]][n]
        return x_copy(j, n, ref, sibling)

    def x_block_arrival(j, n):
        _, prev, nxt, _ = blocks(j, core)
        return x_copy(j, n, kv.at[(prev, nxt)[n]], sibling)

    def sibling_arrival(j, n):
        return x_copy(j, 6 + n, kv.at[blocks(j, 1 - core)[n]], sibling)

    def gather_start(j):
        @pl.when(j <= y)
        def _():
            x_send_copy(j, 0).start()
            if j == 0:
                x_send_copy(j, 3).start()
                v_copy.wait()
                for n in range(4):
                    part_rows = pl.ds(HD * n, HD)
                    kv[c, 1, part_rows] = v_ref[part_rows, :].T
            x_send_copy(j, 1).start()
            if j == 0:
                x_send_copy(j, 2).start()
                k_copy.wait()
                w_copy.start()
                res_copy.start()
            x_send_copy(j, 6).start()

    def gather_forward():
        x_arrival(0, 0).wait_recv()
        x_send_copy(0, 4).start()
        x_arrival(0, 1).wait_recv()
        x_send_copy(0, 5).start()

    def gather_share(j):
        @pl.when(j <= y)
        def _():
            if j == 0:
                x_arrival(j, 2).wait_recv()
            else:
                x_block_arrival(j, 0).wait_recv()
            x_send_copy(j, 7).start()
            if j == 0:
                x_arrival(j, 3).wait_recv()
            else:
                x_block_arrival(j, 1).wait_recv()
            x_send_copy(j, 8).start()
            if j == 0:
                x_arrival(j, 4).wait_recv()
                x_arrival(j, 5).wait_recv()
            elif j < 3:
                y_wait(1, y - j)
            x_send_copy(j, 9).start()

    gather_start(0)
    y_start(0)

    def stacked(quarters, g):
        rows = []
        for r in quarters:
            for h in range(HEADS):
                for u in (2 * g, 2 * g + 1):
                    start = pl.multiple_of(64 * u + 16 * r, 16)
                    rows.append(q_ref[pl.ds(start, 16), h * HD:(h + 1) * HD])
        return jnp.concatenate(rows, axis=0)

    def scores(qs, keys):
        return lax.dot_general(qs, keys, (((1,), (1,)), ((), ())), preferred_element_type=jnp.float32)

    def values(b, first, last):
        return jnp.concatenate([kv[b, 1, HD * n:HD * (n + 1)] for n in range(first, last)], axis=1)

    def own_attention():
        a = lax.broadcasted_iota(jnp.int32, (128, BLK), 1)
        token = 64 * (lax.rem(a, 32) // 16) + 16 * (a // 128) + lax.rem(a, 16)
        key = lax.broadcasted_iota(jnp.int32, (128, BLK), 0)
        for g in range(4):
            qs = stacked(range(4), g)
            last, before = pl.ds(128 * g, 128), pl.ds(0, 128 * g)
            s = jnp.where(key <= token, scores(kv[c, 0, last], qs), NEG)
            m = jnp.max(s, axis=0, keepdims=True)
            if g > 0:
                s_before = scores(kv[c, 0, before], qs)
                m = jnp.maximum(m, jnp.max(s_before, axis=0, keepdims=True))
            p = jnp.exp2((s - m) * EXP2)
            total = jnp.sum(p, axis=0, keepdims=True)
            acc = jnp.dot(values(c, g, g + 1), p.astype(jnp.bfloat16), preferred_element_type=jnp.float32)
            if g > 0:
                p = jnp.exp2((s_before - m) * EXP2)
                total = total + jnp.sum(p, axis=0, keepdims=True)
                acc = acc + jnp.dot(values(c, 0, g), p.astype(jnp.bfloat16), preferred_element_type=jnp.float32)
            own_max[g] = m
            own_sum[g] = total
            own_acc[g] = acc

    q_copy.wait()
    own_attention()

    def a_copy(r):
        return remote(att_send.at[r], att_in.at[y], a_send.at[r], a_recv.at[y], row(r))

    def a_arrival(k):
        return remote(att_in.at[k], att_in.at[k], a_send.at[0], a_recv.at[k], row(lax.rem(y + 1, NY)))

    def far_attention():
        def wait_layer(j, carry):
            for n in range(4):
                sibling_arrival(j, n).wait_recv()
            return carry

        lax.fori_loop(0, y + 1, wait_layer, 0)

        def far_pair(step, carry):
            pair = lax.rem(y // 2 + 1 + step, 2)
            quarters = [2 * pair, 2 * pair + 1]
            rows = pl.ds(pl.multiple_of(256 * pair, 256), 256)

            def group_scores(g):
                qs = stacked(quarters, g)
                return [scores(kv[choice[1 + e, 0, 128 * g], 0], qs) for e in range(2)]

            later = group_scores(0)
            for g in range(4):
                s = later
                if g < 3:
                    later = group_scores(g + 1)
                chosen = [choice[1 + e, 0, 128 * g] for e in range(2)]
                bias = [jnp.where(b != c, 0.0, NEG).astype(jnp.float32) for b in chosen]
                m_own = own_max[g, :, rows]
                m = m_own
                for e in range(2):
                    m = jnp.maximum(m, jnp.max(s[e], axis=0, keepdims=True) + bias[e])
                scale = jnp.exp2((m_own - m) * EXP2)
                total = own_sum[g, :, rows] * scale
                acc = own_acc[g, :, rows] * scale
                for e in range(2):
                    p = jnp.exp2((s[e] - (m - bias[e])) * EXP2)
                    total = total + jnp.sum(p, axis=0, keepdims=True)
                    acc = acc + jnp.dot(
                        values(chosen[e], 0, 4), p.astype(jnp.bfloat16), preferred_element_type=jnp.float32
                    )
                result = (acc * (1.0 / total)).T.astype(jnp.bfloat16)
                to = pl.ds(32 * g, 32)
                for n, r in enumerate(quarters):
                    for h in range(HEADS):
                        first = 128 * n + 32 * h
                        att_send[r, to, h * HD:(h + 1) * HD] = result[first:first + 32]
            for r in quarters:
                @pl.when(r != y)
                def _():
                    a_copy(r).start()

                @pl.when(r == y)
                def _():
                    att_in[y] = att_send[r]
            return carry

        lax.fori_loop(0, 2, far_pair, 0)

    ways = [core, 1 - core]

    def r_copy(n, way, stage, src, dst):
        return remote(src, dst, r_send.at[n, way, stage], r_recv.at[n, way, stage],
                      (c, lax.rem(z + 1 + (NZ - 2) * way, NZ)))

    def shard(step):
        return lax.rem(z + step, NZ)

    def stage_0(n):
        k, h = n // PER_ROW, lax.rem(n, PER_ROW)

        @pl.when((h == 0) & (k != y))
        def _():
            a_arrival(k).wait_recv()

        columns = pl.ds(pl.multiple_of(h * HALF, HALF), HALF)
        product = jnp.dot(att_in[k], w[:, columns], preferred_element_type=jnp.float32)
        part[n] = product.astype(jnp.bfloat16).reshape(NZ, 16, HALF)
        for way in ways:
            columns = pl.ds(pl.multiple_of(way * QUART, QUART), QUART)
            r_copy(n, way, 0, part.at[n, shard(4), :, columns], rin0.at[n, way]).start()

    def stage_1(n):
        for way in ways:
            d = shard(3 + 2 * way)
            columns = pl.ds(pl.multiple_of(way * QUART, QUART), QUART)
            r_copy(n, way, 0, rin0.at[n, way], rin0.at[n, way]).wait_recv()
            total = part[n, d, :, columns].astype(jnp.float32) + rin0[n, way].astype(jnp.float32)
            part[n, d, :, columns] = total.astype(jnp.bfloat16)
            r_copy(n, way, 1, part.at[n, d], rin.at[n, way, 0]).start()

    def stage_mid(n, stage):
        for way in ways:
            d = shard(4 - stage + 2 * stage * way)
            r_copy(n, way, stage - 1, rin.at[n, way, stage - 2], rin.at[n, way, stage - 2]).wait_recv()
            total = part[n, d].astype(jnp.float32) + rin[n, way, stage - 2].astype(jnp.float32)
            part[n, d] = total.astype(jnp.bfloat16)
            r_copy(n, way, stage, part.at[n, d], rin.at[n, way, stage - 1]).start()

    def f_copy(k, h):
        return remote(fin_send.at[k, h], fin_in.at[y, h], f_send.at[k, h], f_recv.at[y, h], row(k))

    def f_arrival(r, h):
        return remote(fin_in.at[r, h], fin_in.at[r, h], f_send.at[0, h], f_recv.at[r, h], row(lax.rem(y + 1, NY)))

    def stage_4(n):
        k, h = n // PER_ROW, lax.rem(n, PER_ROW)
        for way in range(2):
            r_copy(n, way, 3, rin.at[n, way, 2], rin.at[n, way, 2]).wait_recv()
        total = part[n, z].astype(jnp.float32) + rin[n, 0, 2].astype(jnp.float32) + rin[n, 1, 2].astype(jnp.float32)
        total = total.astype(jnp.bfloat16)

        @pl.when(k != y)
        def _():
            fin_send[k, h] = total
            f_copy(k, h).start()

        @pl.when(k == y)
        def _():
            fin_in[y, h] = total

    def tick(t):
        for stage, work in ((0, stage_0), (1, stage_1), (2, lambda n: stage_mid(n, 2)),
                            (3, lambda n: stage_mid(n, 3)), (4, stage_4)):
            n = t - SKEW * stage

            @pl.when((n >= 0) & (n < CHUNKS))
            def _():
                work(n)

    gather_forward()

    @pl.when(y >= 1)
    def _():
        y_wait(0, y - 1)
    y_pass_on(0)
    gather_start(1)
    w_copy.wait()
    choice_copy.wait()
    res_copy.wait()

    def round_(step, carry):
        t = step - 1
        tick(t)

        @pl.when(t == -1)
        def _():
            gather_share(0)
            y_start(1)

            @pl.when(y >= 2)
            def _():
                y_wait(0, y - 2)
            gather_start(2)
            gather_start(3)
            gather_share(1)
            y_pass_on(1)

        for j, at in SHARE_AT:
            @pl.when(t == at)
            def _():
                gather_share(j)

        far_at = sum(jnp.where(y == j, at, 0) for j, at in enumerate(FAR_AT))

        @pl.when(t == far_at)
        def _():
            far_attention()
        return carry

    lax.fori_loop(0, CHUNKS + 4 * SKEW + 1, round_, 0)

    for r in range(NY):
        for h in range(PER_ROW):
            @pl.when(y != r)
            def _():
                f_arrival(r, h).wait_recv()
            rows, columns = pl.ds(16 * r, 16), pl.ds(h * HALF, HALF)
            total = res_ref[rows, columns].astype(jnp.float32) + fin_in[r, h].astype(jnp.float32)
            out_ref[rows, columns] = total.astype(jnp.bfloat16)

    for far in range(2):
        @pl.when(y < NY - 1)
        def _():
            y_own(far, 0).wait_send()

        @pl.when(y == 0)
        def _():
            y_own(far, 1).wait_send()

        @pl.when(y >= 2)
        def _():
            y_relay(far).wait_send()
    for j in range(NY):
        @pl.when(j <= y)
        def _():
            for n in range(10) if j == 0 else (0, 1, 6, 7, 8, 9):
                x_send_copy(j, n).wait_send()
    for r in range(NY):
        @pl.when(y != r)
        def _():
            a_copy(r).wait_send()
            for h in range(PER_ROW):
                f_copy(r, h).wait_send()

    def drain_chunk(n, carry):
        for way in range(2):
            r_copy(n, way, 0, rin0.at[n, way], rin0.at[n, way]).wait_send()
            for stage in (1, 2, 3):
                r_copy(n, way, stage, rin.at[n, way, stage - 1], rin.at[n, way, stage - 1]).wait_send()
        return carry

    lax.fori_loop(0, CHUNKS, drain_chunk, 0)


def body(query_rows, key_rows, value_rows, block_choice, out_weight, residual):
    choice = jnp.transpose(block_choice, (0, 1, 4, 3, 2)).reshape(3, 1, BLK)
    q = query_rows.reshape(BLK, HEADS * HD)
    k = key_rows.reshape(BLK, HD)
    v = value_rows.reshape(BLK, HD)
    res = residual.reshape(BLK // NZ, WIDTH)
    vmem, hbm = pl.BlockSpec(memory_space=pltpu.VMEM), pl.BlockSpec(memory_space=pl.ANY)
    bf16, f32 = jnp.bfloat16, jnp.float32
    dma = pltpu.SemaphoreType.DMA
    out = pl.pallas_call(
        kernel,
        out_shape=jax.ShapeDtypeStruct((BLK // NZ, WIDTH), bf16),
        in_specs=[hbm] * 6,
        out_specs=vmem,
        scratch_shapes=[
            pltpu.SMEM((3, 1, BLK), jnp.int32),
            pltpu.VMEM((BLK, HEADS * HD), bf16),
            pltpu.VMEM((BLK, HD), bf16),
            pltpu.VMEM((BLK // NZ, WIDTH), bf16),
            pltpu.VMEM((2 * NX * NY, 2, BLK, HD), bf16),
            pltpu.VMEM((HEADS * HD, WIDTH), bf16),
            pltpu.VMEM((4, HD, BLK), f32),
            pltpu.VMEM((4, 1, BLK), f32),
            pltpu.VMEM((4, 1, BLK), f32),
            pltpu.VMEM((NY, 128, HEADS * HD), bf16),
            pltpu.VMEM((NY, 128, HEADS * HD), bf16),
            pltpu.VMEM((CHUNKS, NZ, 16, HALF), bf16),
            pltpu.VMEM((CHUNKS, 2, 16, QUART), bf16),
            pltpu.VMEM((CHUNKS, 2, 3, 16, HALF), bf16),
            pltpu.VMEM((NY, PER_ROW, 16, HALF), bf16),
            pltpu.VMEM((NY, PER_ROW, 16, HALF), bf16),
            dma((6,)), dma((2, 3)), dma((2, NY)), dma((NY, 10)), dma((NY, 10)), dma((NY,)), dma((NY,)),
            dma((CHUNKS, 2, 4)), dma((CHUNKS, 2, 4)), dma((NY, PER_ROW)), dma((NY, PER_ROW)),
        ],
        compiler_params=pltpu.CompilerParams(
            collective_id=1, has_side_effects=True, vmem_limit_bytes=62 * 1024 * 1024
        ),
        name="attention_mix",
    )(choice, q, k, v, out_weight, res)
    return out.reshape(1, 1, BLK // NZ, WIDTH)


def solution(mesh):
    placed = (
        P(None, "ctx", None, "tp"),
        P(None, "ctx", None, "tp"),
        P(None, "ctx", None, "tp"),
        P(None, "ctx", None, "tp", None),
        P("tp", None),
        P(None, "ctx", "tp", None),
    )
    return jax.shard_map(
        body, mesh=mesh, in_specs=placed, out_specs=P(None, "ctx", "tp", None), check_vma=False
    )
```

```python
import functools
import math

import jax
import jax.numpy as jnp
from jax import lax
from jax.experimental import pallas as pl
from jax.experimental.pallas import tpu as pltpu
from jax.sharding import PartitionSpec as P

MESH = pl.DeviceIdType.MESH
HD = 128
HEADS = 4
BLK = 512
NX, NY, NZ = 4, 4, 8
WIDTH = 4096
CHUNKS = 8
PER_ROW = CHUNKS // NY
HALF = WIDTH // PER_ROW
QUART = HALF // 2
SKEW = 1
NEG = -1e30
SHARE_AT = ((2, 1), (3, 2))
FAR_AT = (-1, -1, 1, 3)
EXP2 = math.log2(math.e) / math.sqrt(HD)


def kernel(
    choice_hbm, q_hbm, k_hbm, v_hbm, w_hbm, res_hbm, out_ref,
    choice, q_ref, v_ref, res_ref, kv, w, own_acc, own_max, own_sum, att_send, att_in, part, rin0, rin, fin_send, fin_in,
    in_sem, y_send, y_recv, x_send, x_recv, a_send, a_recv, r_send, r_recv, f_send, f_recv,
):
    c = lax.axis_index("ctx")
    z = lax.axis_index("tp")
    core = lax.rem(c, 2)
    x = lax.rem(c // 2, NX)
    y = c // (2 * NX)

    def index(xx, yy, cc):
        return (yy * NX + xx) * 2 + cc

    x_next, x_prev = lax.rem(x + 1, NX), lax.rem(x + NX - 1, NX)
    x_far = lax.rem(x + 2, NX)
    right = (index(x_next, y, core), z)
    left = (index(x_prev, y, core), z)
    sibling = (index(x, y, 1 - core), z)
    up = (c, lax.rem(z + 1, NZ))
    down = (c, lax.rem(z + NZ - 1, NZ))

    def row(yy):
        return (index(x, yy, core), z)

    def remote(src, dst, s_sem, r_sem, device):
        return pltpu.make_async_remote_copy(
            src_ref=src, dst_ref=dst, send_sem=s_sem, recv_sem=r_sem, device_id=device, device_id_type=MESH
        )

    barrier = pltpu.get_barrier_semaphore()
    for device in (right, left, sibling, up, down):
        pl.semaphore_signal(barrier, inc=1, device_id=device, device_id_type=MESH)
    for step in range(1, NY):
        pl.semaphore_signal(barrier, inc=1, device_id=row(lax.rem(y + step, NY)), device_id_type=MESH)
    k_copy, v_copy, q_copy, w_copy, choice_copy, res_copy = [
        pltpu.make_async_copy(src, dst, in_sem.at[n])
        for n, (src, dst) in enumerate(
            [(k_hbm, kv.at[c, 0]), (v_hbm, v_ref), (q_hbm, q_ref), (w_hbm, w), (choice_hbm, choice),
             (res_hbm, res_ref)]
        )
    ]
    for copy in (k_copy, v_copy, q_copy, choice_copy):
        copy.start()
    pl.semaphore_wait(barrier, 8)

    def y_copy(far, n, layer, target):
        b = index(x_far if far else x, layer, core)
        return remote(kv.at[b], kv.at[b], y_send.at[far, n], y_recv.at[far, layer], row(target))

    def y_own(far, n):
        return y_copy(far, n, y, lax.rem(y + 1, NY) if n == 0 else NY - 1)

    def y_relay(far):
        return y_copy(far, 2, lax.rem(NY + 3 - y, NY), lax.rem(NY + 5 - y, NY))

    def y_wait(far, layer):
        y_copy(far, 0, layer, lax.rem(y + 1, NY)).wait_recv()

    def y_start(far):
        @pl.when(y < NY - 1)
        def _():
            y_own(far, 0).start()

        @pl.when(y == 0)
        def _():
            y_own(far, 1).start()

    def y_pass_on(far):
        @pl.when(y == 3)
        def _():
            y_wait(far, 0)

        @pl.when(y >= 2)
        def _():
            y_relay(far).start()

    def blocks(j, cc):
        layer = y - j
        return [index(xx, layer, cc) for xx in (x, x_prev, x_next, x_far)]

    def x_copy(j, n, src, device):
        return remote(src, src, x_send.at[j, n], x_recv.at[j, n], device)

    def x_send_copy(j, n):
        mine, prev, nxt, far = blocks(j, core)
        if n < 4 and j == 0:
            src, half = (k_hbm, 0) if n in (0, 3) else (kv.at[mine, 1], 1)
            device = right if n in (0, 2) else left
            return remote(src, kv.at[mine, half], x_send.at[0, n], x_recv.at[0, n], device)
        src, device = [
            (kv.at[mine], right), (kv.at[mine], left), None, None,
            (kv.at[prev, 0], right), (kv.at[nxt, 1], left),
            (kv.at[mine], sibling), (kv.at[prev], sibling), (kv.at[nxt], sibling), (kv.at[far], sibling),
        ][n]
        return x_copy(j, n, src, device)

    def x_arrival(j, n):
        mine, prev, nxt, far = blocks(j, core)
        ref = [kv.at[prev, 0], kv.at[nxt, 1], kv.at[prev, 1], kv.at[nxt, 0], kv.at[far, 0], kv.at[far, 1]][n]
        return x_copy(j, n, ref, sibling)

    def x_block_arrival(j, n):
        _, prev, nxt, _ = blocks(j, core)
        return x_copy(j, n, kv.at[(prev, nxt)[n]], sibling)

    def sibling_arrival(j, n):
        return x_copy(j, 6 + n, kv.at[blocks(j, 1 - core)[n]], sibling)

    def gather_start(j):
        @pl.when(j <= y)
        def _():
            x_send_copy(j, 0).start()
            if j == 0:
                x_send_copy(j, 3).start()
                v_copy.wait()
                for n in range(4):
                    part_rows = pl.ds(HD * n, HD)
                    kv[c, 1, part_rows] = v_ref[part_rows, :].T
            x_send_copy(j, 1).start()
            if j == 0:
                x_send_copy(j, 2).start()
                k_copy.wait()
                w_copy.start()
                res_copy.start()
            x_send_copy(j, 6).start()

    def gather_forward():
        x_arrival(0, 0).wait_recv()
        x_send_copy(0, 4).start()
        x_arrival(0, 1).wait_recv()
        x_send_copy(0, 5).start()

    def gather_share(j):
        @pl.when(j <= y)
        def _():
            if j == 0:
                x_arrival(j, 2).wait_recv()
            else:
                x_block_arrival(j, 0).wait_recv()
            x_send_copy(j, 7).start()
            if j == 0:
                x_arrival(j, 3).wait_recv()
            else:
                x_block_arrival(j, 1).wait_recv()
            x_send_copy(j, 8).start()
            if j == 0:
                x_arrival(j, 4).wait_recv()
                x_arrival(j, 5).wait_recv()
            elif j < 3:
                y_wait(1, y - j)
            x_send_copy(j, 9).start()

    gather_start(0)
    y_start(0)

    def stacked(quarters, g):
        rows = []
        for r in quarters:
            for h in range(HEADS):
                for u in (2 * g, 2 * g + 1):
                    start = pl.multiple_of(64 * u + 16 * r, 16)
                    rows.append(q_ref[pl.ds(start, 16), h * HD:(h + 1) * HD])
        return jnp.concatenate(rows, axis=0)

    def scores(qs, keys):
        return lax.dot_general(qs, keys, (((1,), (1,)), ((), ())), preferred_element_type=jnp.float32)

    def values(b, first, last):
        return jnp.concatenate([kv[b, 1, HD * n:HD * (n + 1)] for n in range(first, last)], axis=1)

    def own_attention():
        a = lax.broadcasted_iota(jnp.int32, (128, BLK), 1)
        token = 64 * (lax.rem(a, 32) // 16) + 16 * (a // 128) + lax.rem(a, 16)
        key = lax.broadcasted_iota(jnp.int32, (128, BLK), 0)
        for g in range(4):
            qs = stacked(range(4), g)
            last, before = pl.ds(128 * g, 128), pl.ds(0, 128 * g)
            s = jnp.where(key <= token, scores(kv[c, 0, last], qs), NEG)
            m = jnp.max(s, axis=0, keepdims=True)
            if g > 0:
                s_before = scores(kv[c, 0, before], qs)
                m = jnp.maximum(m, jnp.max(s_before, axis=0, keepdims=True))
            p = jnp.exp2((s - m) * EXP2)
            total = jnp.sum(p, axis=0, keepdims=True)
            acc = jnp.dot(values(c, g, g + 1), p.astype(jnp.bfloat16), preferred_element_type=jnp.float32)
            if g > 0:
                p = jnp.exp2((s_before - m) * EXP2)
                total = total + jnp.sum(p, axis=0, keepdims=True)
                acc = acc + jnp.dot(values(c, 0, g), p.astype(jnp.bfloat16), preferred_element_type=jnp.float32)
            own_max[g] = m
            own_sum[g] = total
            own_acc[g] = acc

    q_copy.wait()
    own_attention()

    def a_copy(r):
        return remote(att_send.at[r], att_in.at[y], a_send.at[r], a_recv.at[y], row(r))

    def a_arrival(k):
        return remote(att_in.at[k], att_in.at[k], a_send.at[0], a_recv.at[k], row(lax.rem(y + 1, NY)))

    def far_attention():
        def wait_layer(j, carry):
            for n in range(4):
                sibling_arrival(j, n).wait_recv()
            return carry

        lax.fori_loop(0, y + 1, wait_layer, 0)

        def far_pair(step, carry):
            pair = lax.rem(y // 2 + 1 + step, 2)
            quarters = [2 * pair, 2 * pair + 1]
            rows = pl.ds(pl.multiple_of(256 * pair, 256), 256)

            def group_scores(g):
                qs = stacked(quarters, g)
                return [scores(kv[choice[1 + e, 0, 128 * g], 0], qs) for e in range(2)]

            later = group_scores(0)
            for g in range(4):
                s = later
                if g < 3:
                    later = group_scores(g + 1)
                chosen = [choice[1 + e, 0, 128 * g] for e in range(2)]
                bias = [jnp.where(b != c, 0.0, NEG).astype(jnp.float32) for b in chosen]
                m_own = own_max[g, :, rows]
                m = m_own
                for e in range(2):
                    m = jnp.maximum(m, jnp.max(s[e], axis=0, keepdims=True) + bias[e])
                scale = jnp.exp2((m_own - m) * EXP2)
                total = own_sum[g, :, rows] * scale
                acc = own_acc[g, :, rows] * scale
                for e in range(2):
                    p = jnp.exp2((s[e] - (m - bias[e])) * EXP2)
                    total = total + jnp.sum(p, axis=0, keepdims=True)
                    acc = acc + jnp.dot(
                        values(chosen[e], 0, 4), p.astype(jnp.bfloat16), preferred_element_type=jnp.float32
                    )
                result = (acc * (1.0 / total)).T.astype(jnp.bfloat16)
                to = pl.ds(32 * g, 32)
                for n, r in enumerate(quarters):
                    for h in range(HEADS):
                        first = 128 * n + 32 * h
                        att_send[r, to, h * HD:(h + 1) * HD] = result[first:first + 32]
            for r in quarters:
                @pl.when(r != y)
                def _():
                    a_copy(r).start()

                @pl.when(r == y)
                def _():
                    att_in[y] = att_send[r]
            return carry

        lax.fori_loop(0, 2, far_pair, 0)

    ways = [core, 1 - core]

    def r_copy(n, way, stage, src, dst):
        return remote(src, dst, r_send.at[n, way, stage], r_recv.at[n, way, stage],
                      (c, lax.rem(z + 1 + (NZ - 2) * way, NZ)))

    def shard(step):
        return lax.rem(z + step, NZ)

    def stage_0(n):
        k, h = n // PER_ROW, lax.rem(n, PER_ROW)

        @pl.when((h == 0) & (k != y))
        def _():
            a_arrival(k).wait_recv()

        columns = pl.ds(pl.multiple_of(h * HALF, HALF), HALF)
        product = jnp.dot(att_in[k], w[:, columns], preferred_element_type=jnp.float32)
        part[n] = product.astype(jnp.bfloat16).reshape(NZ, 16, HALF)
        for way in ways:
            columns = pl.ds(pl.multiple_of(way * QUART, QUART), QUART)
            r_copy(n, way, 0, part.at[n, shard(4), :, columns], rin0.at[n, way]).start()

    def stage_1(n):
        for way in ways:
            d = shard(3 + 2 * way)
            columns = pl.ds(pl.multiple_of(way * QUART, QUART), QUART)
            r_copy(n, way, 0, rin0.at[n, way], rin0.at[n, way]).wait_recv()
            total = part[n, d, :, columns].astype(jnp.float32) + rin0[n, way].astype(jnp.float32)
            part[n, d, :, columns] = total.astype(jnp.bfloat16)
            r_copy(n, way, 1, part.at[n, d], rin.at[n, way, 0]).start()

    def stage_mid(n, stage):
        for way in ways:
            d = shard(4 - stage + 2 * stage * way)
            r_copy(n, way, stage - 1, rin.at[n, way, stage - 2], rin.at[n, way, stage - 2]).wait_recv()
            total = part[n, d].astype(jnp.float32) + rin[n, way, stage - 2].astype(jnp.float32)
            part[n, d] = total.astype(jnp.bfloat16)
            r_copy(n, way, stage, part.at[n, d], rin.at[n, way, stage - 1]).start()

    def f_copy(k, h):
        return remote(fin_send.at[k, h], fin_in.at[y, h], f_send.at[k, h], f_recv.at[y, h], row(k))

    def f_arrival(r, h):
        return remote(fin_in.at[r, h], fin_in.at[r, h], f_send.at[0, h], f_recv.at[r, h], row(lax.rem(y + 1, NY)))

    def stage_4(n):
        k, h = n // PER_ROW, lax.rem(n, PER_ROW)
        for way in range(2):
            r_copy(n, way, 3, rin.at[n, way, 2], rin.at[n, way, 2]).wait_recv()
        total = part[n, z].astype(jnp.float32) + rin[n, 0, 2].astype(jnp.float32) + rin[n, 1, 2].astype(jnp.float32)
        total = total.astype(jnp.bfloat16)

        @pl.when(k != y)
        def _():
            fin_send[k, h] = total
            f_copy(k, h).start()

        @pl.when(k == y)
        def _():
            fin_in[y, h] = total

    def tick(t):
        for stage, work in ((0, stage_0), (1, stage_1), (2, lambda n: stage_mid(n, 2)),
                            (3, lambda n: stage_mid(n, 3)), (4, stage_4)):
            n = t - SKEW * stage

            @pl.when((n >= 0) & (n < CHUNKS))
            def _():
                work(n)

    gather_forward()

    @pl.when(y >= 1)
    def _():
        y_wait(0, y - 1)
    y_pass_on(0)
    gather_start(1)
    w_copy.wait()
    choice_copy.wait()
    res_copy.wait()

    def round_(step, carry):
        t = step - 1
        tick(t)

        @pl.when(t == -1)
        def _():
            gather_share(0)
            y_start(1)

            @pl.when(y >= 2)
            def _():
                y_wait(0, y - 2)
            gather_start(2)
            gather_start(3)
            gather_share(1)
            y_pass_on(1)

        for j, at in SHARE_AT:
            @pl.when(t == at)
            def _():
                gather_share(j)

        far_at = sum(jnp.where(y == j, at, 0) for j, at in enumerate(FAR_AT))

        @pl.when(t == far_at)
        def _():
            far_attention()
        return carry

    lax.fori_loop(0, CHUNKS + 4 * SKEW + 1, round_, 0)

    for r in range(NY):
        for h in range(PER_ROW):
            @pl.when(y != r)
            def _():
                f_arrival(r, h).wait_recv()
            rows, columns = pl.ds(16 * r, 16), pl.ds(h * HALF, HALF)
            total = res_ref[rows, columns].astype(jnp.float32) + fin_in[r, h].astype(jnp.float32)
            out_ref[rows, columns] = total.astype(jnp.bfloat16)

    for far in range(2):
        @pl.when(y < NY - 1)
        def _():
            y_own(far, 0).wait_send()

        @pl.when(y == 0)
        def _():
            y_own(far, 1).wait_send()

        @pl.when(y >= 2)
        def _():
            y_relay(far).wait_send()
    for j in range(NY):
        @pl.when(j <= y)
        def _():
            for n in range(10) if j == 0 else (0, 1, 6, 7, 8, 9):
                x_send_copy(j, n).wait_send()
    for r in range(NY):
        @pl.when(y != r)
        def _():
            a_copy(r).wait_send()
            for h in range(PER_ROW):
                f_copy(r, h).wait_send()

    def drain_chunk(n, carry):
        for way in range(2):
            r_copy(n, way, 0, rin0.at[n, way], rin0.at[n, way]).wait_send()
            for stage in (1, 2, 3):
                r_copy(n, way, stage, rin.at[n, way, stage - 1], rin.at[n, way, stage - 1]).wait_send()
        return carry

    lax.fori_loop(0, CHUNKS, drain_chunk, 0)


def body(query_rows, key_rows, value_rows, block_choice, out_weight, residual):
    choice = jnp.transpose(block_choice, (0, 1, 4, 3, 2)).reshape(3, 1, BLK)
    q = query_rows.reshape(BLK, HEADS * HD)
    k = key_rows.reshape(BLK, HD)
    v = value_rows.reshape(BLK, HD)
    res = residual.reshape(BLK // NZ, WIDTH)
    vmem, hbm = pl.BlockSpec(memory_space=pltpu.VMEM), pl.BlockSpec(memory_space=pl.ANY)
    bf16, f32 = jnp.bfloat16, jnp.float32
    dma = pltpu.SemaphoreType.DMA
    out = pl.pallas_call(
        kernel,
        out_shape=jax.ShapeDtypeStruct((BLK // NZ, WIDTH), bf16),
        in_specs=[hbm] * 6,
        out_specs=vmem,
        scratch_shapes=[
            pltpu.SMEM((3, 1, BLK), jnp.int32),
            pltpu.VMEM((BLK, HEADS * HD), bf16),
            pltpu.VMEM((BLK, HD), bf16),
            pltpu.VMEM((BLK // NZ, WIDTH), bf16),
            pltpu.VMEM((2 * NX * NY, 2, BLK, HD), bf16),
            pltpu.VMEM((HEADS * HD, WIDTH), bf16),
            pltpu.VMEM((4, HD, BLK), f32),
            pltpu.VMEM((4, 1, BLK), f32),
            pltpu.VMEM((4, 1, BLK), f32),
            pltpu.VMEM((NY, 128, HEADS * HD), bf16),
            pltpu.VMEM((NY, 128, HEADS * HD), bf16),
            pltpu.VMEM((CHUNKS, NZ, 16, HALF), bf16),
            pltpu.VMEM((CHUNKS, 2, 16, QUART), bf16),
            pltpu.VMEM((CHUNKS, 2, 3, 16, HALF), bf16),
            pltpu.VMEM((NY, PER_ROW, 16, HALF), bf16),
            pltpu.VMEM((NY, PER_ROW, 16, HALF), bf16),
            dma((6,)), dma((2, 3)), dma((2, NY)), dma((NY, 10)), dma((NY, 10)), dma((NY,)), dma((NY,)),
            dma((CHUNKS, 2, 4)), dma((CHUNKS, 2, 4)), dma((NY, PER_ROW)), dma((NY, PER_ROW)),
        ],
        compiler_params=pltpu.CompilerParams(
            collective_id=1, has_side_effects=True, vmem_limit_bytes=62 * 1024 * 1024
        ),
        name="attention_mix",
    )(choice, q, k, v, out_weight, res)
    return out.reshape(1, 1, BLK // NZ, WIDTH)


def solution(mesh):
    placed = (
        P(None, "ctx", None, "tp"),
        P(None, "ctx", None, "tp"),
        P(None, "ctx", None, "tp"),
        P(None, "ctx", None, "tp", None),
        P("tp", None),
        P(None, "ctx", "tp", None),
    )
    return jax.shard_map(
        body, mesh=mesh, in_specs=placed, out_specs=P(None, "ctx", "tp", None), check_vma=False
    )
```
